512 devices in a mesh: rep: 128 (over z, y, core), shard: 4 (over x).
Axes of the slice: x: 4, y: 8, z: 8, core: 2. Of those that a mesh axis runs over, the one named last changes fastest.
Arguments:
- grad_query: bfloat16 [128, 128, 8192], P('rep', 'shard'), may hold values from -24 to 24
- error_query: bfloat16 [128, 128, 8192], P('rep', 'shard'), may hold values from -4 to 4
- q_query: float32 [64, 8192], P(None, ('rep', 'shard')), may hold values from -6 to 6
- grad_down: bfloat16 [128, 256, 8192], P('rep', 'shard'), may hold values from -24 to 24
- error_down: bfloat16 [128, 256, 8192], P('rep', 'shard'), may hold values from -4 to 4
- q_down: float32 [64, 8192], P(None, ('rep', 'shard')), may hold values from -6 to 6
Outputs:
- error_query_new: bfloat16 [128, 128, 8192], P('rep', 'shard')
- basis_query: float32 [128, 64], P('shard')
- q_query_new: float32 [64, 8192], P(None, ('rep', 'shard'))
- error_down_new: bfloat16 [128, 256, 8192], P('rep', 'shard')
- basis_down: float32 [256, 64], P('shard')
- q_down_new: float32 [64, 8192], P(None, ('rep', 'shard'))
The draws below stay inside these ranges and needn't reach their ends.
All inputs are finite; a program needn't handle non-finite values.
Results may differ from the reference program's by a relative error of at most 0.001.
Values sent between devices are 32-bit elements; how exact they have to be, the bound alone decides.
No kernel may reach another device: no remote copies, remote signals or barrier semaphores. Data moves between devices by JAX's collectives and lax.ppermute only.
A program may use at most 64 MiB of HBM per device.

```python
import jax
import jax.numpy as jnp
from jax import lax

D = 8192
RANK = 64
REPLICAS = 128
QP_ROWS = 128
DN_ROWS = 256


def with_spikes(entries, key, source, target, shards_of, factor):
    def block_of(axis_at):
        return (jnp.arange(entries.shape[axis_at]) // (entries.shape[axis_at] // shards_of)).reshape((-1,) + (1,) * (entries.ndim - 1 - axis_at))

    near = jax.random.permutation(key, shards_of)[block_of(target)]
    second = (block_of(target) + shards_of // 2) % shards_of
    return jnp.where((block_of(source) == near) | (block_of(source) == second), factor * entries, entries)


def shard_levels(stream_key, shape, split, low, high):
    loudness, own = 1.0, jax.random.fold_in(stream_key, 6)
    for axis_at, blocks in split:
        draws = jnp.exp(jax.random.uniform(jax.random.fold_in(own, axis_at), (blocks,), jnp.float32, low / len(split), high / len(split)))
        loudness = loudness * jnp.repeat(draws, shape[axis_at] // blocks).reshape([-1 if axis == axis_at else 1 for axis in range(len(shape))])
    return loudness


def normal_values(rng, extent, width, bound, shards=(), kind=jnp.bfloat16):
    factor_of = shard_levels(rng, extent, shards, -0.22, 0.18) if shards else 1.0
    result = jax.random.normal(rng, extent, jnp.float32) * width * factor_of
    return jnp.minimum(jnp.maximum(result, -bound), bound).astype(kind)


def noise_with(rng, dims, scale, limit, shards, heavy, kind=jnp.bfloat16):
    drawn = scale * jax.random.normal(rng, dims, jnp.float32)
    if shards:
        drawn = drawn * shard_levels(rng, dims, shards, -0.22, 0.18)
    return jnp.clip(with_spikes(drawn, jax.random.fold_in(rng, 3), *heavy), -limit, limit).astype(kind)


def setup_inputs(seed: int = 0) -> dict:
    arg_keys = jax.random.split(jax.random.key(seed), 7)
    return {
        "grad_query": noise_with(arg_keys[0], (REPLICAS, QP_ROWS, D), 1.0, 24.0, ((0, 128), (1, 4)), (0, 2, 128, 5.5)),
        "error_query": normal_values(arg_keys[1], (REPLICAS, QP_ROWS, D), 0.5, 4.0, ((0, 128), (1, 4))),
        "q_query": normal_values(arg_keys[2], (RANK, D), 1.0, 6.0, ((1, 512),), jnp.float32),
        "grad_down": noise_with(arg_keys[3], (REPLICAS, DN_ROWS, D), 1.0, 24.0, ((0, 128), (1, 4)), (0, 2, 128, 5.5)),
        "error_down": normal_values(arg_keys[4], (REPLICAS, DN_ROWS, D), 0.5, 4.0, ((0, 128), (1, 4))),
        "q_down": normal_values(arg_keys[5], (RANK, D), 1.0, 6.0, ((1, 512),), jnp.float32),
    }


def compress(grad, error, q_old):
    high = lax.Precision.HIGHEST
    summed = jnp.sum(grad, axis=0, dtype=jnp.float32) + jnp.sum(error, axis=0, dtype=jnp.float32)
    factor = jnp.dot(summed, q_old.T, precision=high)
    gram = jnp.dot(factor.T, factor, precision=high)
    lower = jnp.linalg.cholesky(gram)
    basis = jax.scipy.linalg.solve_triangular(lower, factor.T, lower=True).T
    q_new = jnp.dot(basis.T, summed, precision=high) / REPLICAS
    approx = jnp.dot(basis, q_new, precision=high)

    def one_replica(pair):
        return (pair[0].astype(jnp.float32) + pair[1].astype(jnp.float32) - approx).astype(jnp.bfloat16)
    new_error = lax.map(one_replica, (grad, error))
    return (new_error, basis, q_new)

def reference(grad_query, error_query, q_query, grad_down, error_down, q_down):
    error_query_new, basis_query, q_query_new = compress(grad_query, error_query, q_query)
    error_down_new, basis_down, q_down_new = compress(grad_down, error_down, q_down)
    return (error_query_new, basis_query, q_query_new, error_down_new, basis_down, q_down_new)
```

```python
import jax
import jax.numpy as jnp
from jax import lax
from jax.experimental import pallas as pl
from jax.experimental.pallas import tpu as pltpu
from jax.sharding import Mesh, PartitionSpec as P

NZ, NY, NC, NX = 8, 8, 2, 4
AXES = ("z", "y", "core", "x")
RANK = 64
LANES = 128
QH, DH = 16, 32
HALF = QH + DH
PACK = HALF // 2
HIGH = lax.Precision.HIGHEST
PARAMS = pltpu.CompilerParams(vmem_limit_bytes=40 * 1024 * 1024)


def device_of(z, y, core, x):
    return ((z * NY + y) * NC + core) * NX + x


def split_groups(core_along_y):
    groups = []
    for core in range(NC):
        for x in range(NX):
            for fixed in range(8):
                if core == core_along_y:
                    groups.append([device_of(fixed, v, core, x) for v in range(8)])
                else:
                    groups.append([device_of(v, fixed, core, x) for v in range(8)])
    return groups


WIDE = split_groups(0)
NARROW = split_groups(1)


def exchange(x, groups):
    return lax.all_to_all(x, AXES, 0, 0, axis_index_groups=groups, tiled=True)


def column_of(core, i, j):
    block = jnp.where(core == 0, j * NY + i, i * NY + j)
    return pl.multiple_of(block * LANES, LANES)


def merge_kernel(core_ref, gq, eq, gd, ed, qq, qd, send, keep, qpack):
    core = core_ref[0]
    f32 = jnp.float32
    for out, owner in ((send, 1 - core), (keep, core)):
        rq = pl.ds(pl.multiple_of(owner * QH, QH), QH)
        rd = pl.ds(pl.multiple_of(owner * DH, DH), DH)
        for i in range(8):
            for j in range(8):
                cols = pl.ds(column_of(owner, i, j), LANES)
                out[i, j, 0:QH, :] = gq[rq, cols].astype(f32) + eq[rq, cols].astype(f32)
                out[i, j, QH:HALF, :] = gd[rd, cols].astype(f32) + ed[rd, cols].astype(f32)
    qpack[...] = jnp.concatenate([qq[...], qd[...]], axis=1)


def factor_kernel(parts, qpack, s_ref, f_ref):
    s = parts[0]
    for i in range(1, 8):
        s = s + parts[i]
    s_ref[...] = s
    r = jnp.dot(s, qpack[...], precision=HIGH, preferred_element_type=jnp.float32)
    low = jnp.concatenate([r[0:QH], pltpu.roll(r[40:48], RANK, 1)], axis=0)
    lane = lax.broadcasted_iota(jnp.int32, (PACK, LANES), 1)
    packed = jnp.where(lane < RANK, low, r[QH:40])
    for i in range(8):
        f_ref[i] = packed


def unpack_factor(p):
    lane_q = lax.broadcasted_iota(jnp.int32, (QH, LANES), 1)
    lane_d = lax.broadcasted_iota(jnp.int32, (DH, LANES), 1)
    fq = jnp.where(lane_q < RANK, p[0:QH], 0.0)
    fd = jnp.where(lane_d >= RANK, jnp.concatenate([p, pltpu.roll(p[QH:PACK], RANK, 1)], axis=0), 0.0)
    return fq, fd


def inverse_lower(gram):
    row = lax.broadcasted_iota(jnp.int32, (8, LANES), 0)
    lane = lax.broadcasted_iota(jnp.int32, (8, LANES), 1)
    nb = RANK // 8
    q, d = [], []
    for b in range(nb):
        eye_q = jnp.where(lane - RANK == row + 8 * b, 1.0, 0.0)
        eye_d = jnp.where(lane == row + 8 * b, 1.0, 0.0)
        q.append(jnp.where(lane < RANK, gram[8 * b:8 * b + 8], eye_q))
        d.append(jnp.where(lane >= RANK, gram[RANK + 8 * b:RANK + 8 * b + 8], eye_d))
    for k in range(RANK):
        b0, s = divmod(k, 8)
        for m, at in ((q, k), (d, RANK + k)):
            inv = lax.rsqrt(m[b0][s:s + 1, at:at + 1])
            top = m[b0][s:s + 1, :] * inv
            for b in range(b0, nb):
                col = m[b][:, at:at + 1] * inv
                if b == b0:
                    col = jnp.where(row > s, col, 0.0)
                    m[b] = jnp.where(row == s, top, m[b] - col * top)
                else:
                    m[b] = m[b] - col * top
    zero = jnp.zeros((8, LANES), jnp.float32)
    out = [jnp.where(lane < RANK, pltpu.roll(m, RANK, 1), zero) for m in q]
    out += [jnp.where(lane >= RANK, pltpu.roll(m, RANK, 1), zero) for m in d]
    return jnp.concatenate(out, axis=0)


def contract(a, b, dims):
    return lax.dot_general(a, b, (dims, ((), ())), precision=HIGH, preferred_element_type=jnp.float32)


def solve_kernel(where_ref, all_ref, basis_q, basis_d, qn_q, qn_d, approx, qn_scratch):
    core, x = where_ref[0], where_ref[1]
    f_rows, s_rows = [], []
    for g in range(8):
        fq, fd = unpack_factor(all_ref[g, 0:PACK])
        f_rows += [fq, fd]
        s_rows.append(all_ref[g, PACK:PACK + HALF])
    f = jnp.concatenate(f_rows, axis=0)
    s = jnp.concatenate(s_rows, axis=0)
    rows = ((0,), (0,))
    lanes = ((1,), (1,))
    gram = contract(f, f, rows)
    cross = contract(s, f, rows)
    inv = inverse_lower(gram)
    qn = contract(cross, inv, lanes) * (1.0 / (NZ * NY * NC))
    qn_scratch[0] = qn
    qn_scratch[1] = pltpu.roll(qn, RANK, 1)
    own = pl.ds(pl.multiple_of(core * 64 + x * 16, 16), 16)
    qn_q[...] = qn_scratch[0, own, 0:RANK]
    qn_d[...] = qn_scratch[1, own, 0:RANK]
    halves = []
    for c in range(NC):
        fq, fd = unpack_factor(all_ref[c * NX + x, 0:PACK])
        b = contract(jnp.concatenate([fq, fd], axis=0), inv, lanes)
        halves.append(b)
        basis_q[c * QH:(c + 1) * QH, :] = b[0:QH, 0:RANK]
        basis_d[c * DH:(c + 1) * DH, :] = pltpu.roll(b[QH:HALF], RANK, 1)[:, 0:RANK]
    mine = jnp.where(core == 0, halves[0], halves[1])
    a = contract(mine, qn, lanes)
    for i in range(8):
        approx[i] = a


def error_kernel(core_ref, gq, eq, gd, ed, own, other, out_q, out_d):
    core = core_ref[0]
    f32 = jnp.float32
    for src, owner in ((own, core), (other, 1 - core)):
        rq = pl.ds(pl.multiple_of(owner * QH, QH), QH)
        rd = pl.ds(pl.multiple_of(owner * DH, DH), DH)
        for i in range(8):
            for j in range(8):
                cols = pl.ds(column_of(owner, i, j), LANES)
                mq = gq[rq, cols].astype(f32) + eq[rq, cols].astype(f32)
                md = gd[rd, cols].astype(f32) + ed[rd, cols].astype(f32)
                out_q[rq, cols] = (mq - src[i, j, 0:QH, :]).astype(jnp.bfloat16)
                out_d[rd, cols] = (md - src[i, j, QH:HALF, :]).astype(jnp.bfloat16)


def shape(*dims, dtype=jnp.float32):
    return jax.ShapeDtypeStruct(dims, dtype)


def call(kernel, n_in, out_shape, scalars=0, scratch=()):
    vmem = pl.BlockSpec(memory_space=pltpu.VMEM)
    smem = pl.BlockSpec(memory_space=pltpu.SMEM)
    return pl.pallas_call(
        kernel,
        out_shape=out_shape,
        in_specs=[smem] * scalars + [vmem] * n_in,
        out_specs=jax.tree.map(lambda _: vmem, out_shape),
        scratch_shapes=list(scratch),
        compiler_params=PARAMS,
    )


def swap_cores(x):
    return lax.ppermute(x, "core", [(0, 1), (1, 0)])


def on_device(grad_query, error_query, q_query, grad_down, error_down, q_down):
    core = lax.axis_index("core").astype(jnp.int32)
    place = jnp.stack([core, lax.axis_index("x").astype(jnp.int32)])
    half = shape(8, 8, HALF, LANES)
    grads = (grad_query[0], error_query[0], grad_down[0], error_down[0])
    send, keep, qpack = call(merge_kernel, 6, (half, half, shape(16, LANES)), 1)(
        place, *grads, q_query.T, q_down.T
    )
    q_all = lax.all_to_all(
        jnp.broadcast_to(qpack[None], (8, 16, LANES)), ("core", "x"), 0, 0, tiled=True
    ).reshape(LANES, LANES)
    part = exchange(keep + swap_cores(send), WIDE)
    part = exchange(jnp.sum(part, axis=0), NARROW)
    s_own, f = call(factor_kernel, 2, (shape(HALF, LANES), shape(8, PACK, LANES)))(part, q_all)
    f = exchange(f, NARROW)
    f = jnp.broadcast_to(jnp.sum(f, axis=0)[None], (8, PACK, LANES))
    f = jnp.sum(exchange(f, WIDE), axis=0)
    both = jnp.concatenate([f, s_own], axis=0)
    both = lax.all_to_all(
        jnp.broadcast_to(both[None], (8, PACK + HALF, LANES)), ("core", "x"), 0, 0, tiled=True
    )
    basis_q, basis_d, qn_q, qn_d, approx = call(
        solve_kernel,
        1,
        (shape(2 * QH, RANK), shape(2 * DH, RANK), shape(16, RANK), shape(16, RANK), shape(8, HALF, LANES)),
        1,
        [pltpu.VMEM((2, LANES, LANES), jnp.float32)],
    )(place, both)
    approx = exchange(approx, NARROW)
    own = exchange(jnp.broadcast_to(approx[None], (8, 8, HALF, LANES)), WIDE)
    other = swap_cores(own)
    err_q, err_d = call(
        error_kernel, 6, (shape(2 * QH, 8192, dtype=jnp.bfloat16), shape(2 * DH, 8192, dtype=jnp.bfloat16)), 1
    )(place, *grads, own, other)
    return (err_q[None], basis_q, qn_q.T, err_d[None], basis_d, qn_d.T)


def solution(mesh):
    torus = Mesh(mesh.devices.reshape(NZ, NY, NC, NX), AXES)
    rep = ("z", "y", "core")
    big = P(rep, "x", None)
    right = P(None, AXES)
    left = P("x", None)
    return jax.shard_map(
        on_device,
        mesh=torus,
        in_specs=(big, big, right, big, big, right),
        out_specs=(big, left, right, big, left, right),
        check_vma=False,
    )
```

```python
import jax
import jax.numpy as jnp
from jax import lax
from jax.experimental import pallas as pl
from jax.experimental.pallas import tpu as pltpu
from jax.sharding import Mesh, PartitionSpec as P

NZ, NY, NC, NX = 8, 8, 2, 4
AXES = ("z", "y", "core", "x")
RANK = 64
LANES = 128
QH, DH = 16, 32
HALF = QH + DH
PACK = HALF // 2
HIGH = lax.Precision.HIGHEST
WIDTH = 8192
CHUNK = 2048
CHUNKS = WIDTH // CHUNK
QPAD = 256
MIB = 1024 * 1024
SEND_VMEM, KEEP_VMEM, FACTOR_VMEM = 62, 59, 63.25


def device_of(z, y, core, x):
    return ((z * NY + y) * NC + core) * NX + x


def split_groups(core_along_y):
    groups = []
    for core in range(NC):
        for x in range(NX):
            for fixed in range(8):
                if core == core_along_y:
                    groups.append([device_of(fixed, v, core, x) for v in range(8)])
                else:
                    groups.append([device_of(v, fixed, core, x) for v in range(8)])
    return groups


WIDE = split_groups(0)
NARROW = split_groups(1)


def exchange(x, groups):
    return lax.all_to_all(x, AXES, 0, 0, axis_index_groups=groups, tiled=True)


def slot(owner, block):
    z, y = divmod(block, NY)
    return jnp.where(owner == 0, y, z), jnp.where(owner == 0, z, y)


def merge_half(owner, sources, bufs, sems, out):
    f32 = jnp.float32
    copies = []
    for ch in range(CHUNKS):
        cols = pl.ds(ch * CHUNK, CHUNK)
        part = []
        for a, (src, buf) in enumerate(zip(sources, bufs)):
            n = buf.shape[0]
            rows = pl.ds(pl.multiple_of(owner * n, n), n)
            part.append(pltpu.make_async_copy(src.at[rows, cols], buf.at[:, cols], sems.at[ch, a]))
        copies.append(part)
        for c in part:
            c.start()
    gq, eq, gd, ed = bufs
    per = CHUNK // LANES
    for ch in range(CHUNKS):
        for c in copies[ch]:
            c.wait()
        for block in range(ch * per, (ch + 1) * per):
            i, j = slot(owner, block)
            cols = pl.ds(block * LANES, LANES)
            out[i, j, 0:QH, :] = gq[:, cols].astype(f32) + eq[:, cols].astype(f32)
            out[i, j, QH:HALF, :] = gd[:, cols].astype(f32) + ed[:, cols].astype(f32)


def send_kernel(core_ref, gq, eq, gd, ed, out, bq, cq, bd, cd, sems):
    merge_half(1 - core_ref[0], (gq, eq, gd, ed), (bq, cq, bd, cd), sems, out)


def keep_kernel(core_ref, gq, eq, gd, ed, qq, qd, out, qpack, bq, cq, bd, cd, sems, qbuf, qsems):
    q_copies = [pltpu.make_async_copy(r, qbuf.at[k], qsems.at[k]) for k, r in enumerate((qq, qd))]
    for c in q_copies:
        c.start()
    qpack[16:QPAD, :] = jnp.zeros((QPAD - 16, LANES), jnp.float32)
    for c in q_copies:
        c.wait()
    qpack[0:16, :] = jnp.concatenate([qbuf[0], qbuf[1]], axis=1)
    merge_half(core_ref[0], (gq, eq, gd, ed), (bq, cq, bd, cd), sems, out)


def factor_kernel(parts, q_all, s_ref, f_ref, qbuf, qsems):
    copies = [pltpu.make_async_copy(q_all.at[g, 0:16], qbuf.at[g], qsems.at[g]) for g in range(8)]
    for c in copies:
        c.start()
    s = parts[0]
    for i in range(1, 8):
        s = s + parts[i]
    s_ref[...] = s
    for c in copies:
        c.wait()
    r = jnp.dot(s, qbuf[...].reshape(LANES, LANES), precision=HIGH, preferred_element_type=jnp.float32)
    low = jnp.concatenate([r[0:QH], pltpu.roll(r[40:48], RANK, 1)], axis=0)
    lane = lax.broadcasted_iota(jnp.int32, (PACK, LANES), 1)
    packed = jnp.where(lane < RANK, low, r[QH:40])
    for i in range(8):
        f_ref[i] = packed


def unpack_factor(p):
    lane_q = lax.broadcasted_iota(jnp.int32, (QH, LANES), 1)
    lane_d = lax.broadcasted_iota(jnp.int32, (DH, LANES), 1)
    fq = jnp.where(lane_q < RANK, p[0:QH], 0.0)
    fd = jnp.where(lane_d >= RANK, jnp.concatenate([p, pltpu.roll(p[QH:PACK], RANK, 1)], axis=0), 0.0)
    return fq, fd


def inverse_lower(gram):
    row = lax.broadcasted_iota(jnp.int32, (8, LANES), 0)
    lane = lax.broadcasted_iota(jnp.int32, (8, LANES), 1)
    nb = RANK // 8
    q, d = [], []
    for b in range(nb):
        eye_q = jnp.where(lane - RANK == row + 8 * b, 1.0, 0.0)
        eye_d = jnp.where(lane == row + 8 * b, 1.0, 0.0)
        q.append(jnp.where(lane < RANK, gram[8 * b:8 * b + 8], eye_q))
        d.append(jnp.where(lane >= RANK, gram[RANK + 8 * b:RANK + 8 * b + 8], eye_d))

    def spread_row(v, s):
        return jnp.broadcast_to(v[s:s + 1, :], (8, LANES))

    def spread_lane(v, at):
        return jnp.broadcast_to(v[:, at:at + 1], (8, LANES))

    for b in range(nb):
        for m, base in ((q, 0), (d, RANK)):
            at = base + 8 * b
            top = m[b]
            col = [spread_lane(top, at + t) for t in range(8)]
            below = [(i, [spread_lane(m[i], at + t) for t in range(8)]) for i in range(b + 1, nb)]
            pivots = jnp.ones((8, LANES), jnp.float32)
            for s in range(8):
                p = spread_row(col[s], s)
                pivots = jnp.where(row == s, p, pivots)
                r = 1.0 / p
                pivot_row = spread_row(top, s)
                upper = {t: spread_row(col[t], s) for t in range(s + 1, 8)}
                f = jnp.where(row > s, col[s] * r, 0.0)
                top = top - f * pivot_row
                for t in upper:
                    col[t] = col[t] - f * upper[t]
                for i, c in below:
                    g = c[s] * r
                    m[i] = m[i] - g * pivot_row
                    for t in upper:
                        c[t] = c[t] - g * upper[t]
            m[b] = top * lax.rsqrt(pivots)
    zero = jnp.zeros((8, LANES), jnp.float32)
    out = [jnp.where(lane < RANK, pltpu.roll(m, RANK, 1), zero) for m in q]
    out += [jnp.where(lane >= RANK, pltpu.roll(m, RANK, 1), zero) for m in d]
    return jnp.concatenate(out, axis=0)


def contract(a, b, dims):
    return lax.dot_general(a, b, (dims, ((), ())), precision=HIGH, preferred_element_type=jnp.float32)


def solve_kernel(where_ref, all_ref, basis_q, basis_d, qn_q, qn_d, approx, qn_scratch):
    core, x = where_ref[0], where_ref[1]
    f_rows, s_rows = [], []
    for g in range(8):
        fq, fd = unpack_factor(all_ref[g, 0:PACK])
        f_rows += [fq, fd]
        s_rows.append(all_ref[g, PACK:PACK + HALF])
    f = jnp.concatenate(f_rows, axis=0)
    s = jnp.concatenate(s_rows, axis=0)
    rows = ((0,), (0,))
    lanes = ((1,), (1,))
    gram = contract(f, f, rows)
    cross = contract(s, f, rows)
    inv = inverse_lower(gram)
    qn = contract(cross, inv, lanes) * (1.0 / (NZ * NY * NC))
    qn_scratch[0] = qn
    qn_scratch[1] = pltpu.roll(qn, RANK, 1)
    own = pl.ds(pl.multiple_of(core * 64 + x * 16, 16), 16)
    qn_q[...] = qn_scratch[0, own, 0:RANK]
    qn_d[...] = qn_scratch[1, own, 0:RANK]
    halves = []
    for c in range(NC):
        fq, fd = unpack_factor(all_ref[c * NX + x, 0:PACK])
        b = contract(jnp.concatenate([fq, fd], axis=0), inv, lanes)
        halves.append(b)
        basis_q[c * QH:(c + 1) * QH, :] = b[0:QH, 0:RANK]
        basis_d[c * DH:(c + 1) * DH, :] = pltpu.roll(b[QH:HALF], RANK, 1)[:, 0:RANK]
    mine = jnp.where(core == 0, halves[0], halves[1])
    a = contract(mine, qn, lanes)
    for i in range(8):
        approx[i] = a


def error_half(owner, gq, eq, gd, ed, src, out_q, out_d, buf_q, buf_d, sems):
    f32 = jnp.float32
    rq = pl.ds(pl.multiple_of(owner * QH, QH), QH)
    rd = pl.ds(pl.multiple_of(owner * DH, DH), DH)
    per = CHUNK // LANES
    copies = []
    for ch in range(CHUNKS):
        for block in range(ch * per, (ch + 1) * per):
            i, j = slot(owner, block)
            cols = pl.ds(block * LANES, LANES)
            mq = gq[rq, cols].astype(f32) + eq[rq, cols].astype(f32)
            md = gd[rd, cols].astype(f32) + ed[rd, cols].astype(f32)
            buf_q[:, cols] = (mq - src[i, j, 0:QH, :]).astype(jnp.bfloat16)
            buf_d[:, cols] = (md - src[i, j, QH:HALF, :]).astype(jnp.bfloat16)
        cols = pl.ds(ch * CHUNK, CHUNK)
        for a, (buf, out, rows) in enumerate(((buf_q, out_q, rq), (buf_d, out_d, rd))):
            c = pltpu.make_async_copy(buf.at[:, cols], out.at[rows, cols], sems.at[ch, a])
            c.start()
            copies.append(c)
    for c in copies:
        c.wait()


def own_error_kernel(core_ref, gq, eq, gd, ed, src, out_q, out_d, buf_q, buf_d, sems):
    error_half(core_ref[0], gq, eq, gd, ed, src, out_q, out_d, buf_q, buf_d, sems)


def other_error_kernel(core_ref, gq, eq, gd, ed, src, in_q, in_d, out_q, out_d, buf_q, buf_d, sems):
    error_half(1 - core_ref[0], gq, eq, gd, ed, src, out_q, out_d, buf_q, buf_d, sems)


def shape(*dims, dtype=jnp.float32):
    return jax.ShapeDtypeStruct(dims, dtype)


VM = pl.BlockSpec(memory_space=pltpu.VMEM)
SM = pl.BlockSpec(memory_space=pltpu.SMEM)
HB = pl.BlockSpec(memory_space=pltpu.HBM)


def call(kernel, in_specs, out_shape, out_specs, scratch=(), moved=0, aliases=None, vmem=24):
    return pl.pallas_call(
        kernel,
        out_shape=out_shape,
        in_specs=in_specs,
        out_specs=out_specs,
        scratch_shapes=list(scratch),
        input_output_aliases=aliases or {},
        cost_estimate=pl.CostEstimate(flops=moved, bytes_accessed=moved, transcendentals=0),
        compiler_params=pltpu.CompilerParams(vmem_limit_bytes=int(vmem * MIB)),
    )


def swap_cores(x):
    return lax.ppermute(x, "core", [(0, 1), (1, 0)])


def on_device(grad_query, error_query, q_query, grad_down, error_down, q_down):
    core = lax.axis_index("core").astype(jnp.int32)
    place = jnp.stack([core, lax.axis_index("x").astype(jnp.int32)])
    half = shape(8, 8, HALF, LANES)
    bf16 = jnp.bfloat16
    dma = pltpu.SemaphoreType.DMA
    half_bufs = [pltpu.VMEM((n, WIDTH), bf16) for n in (QH, QH, DH, DH)] + [dma((CHUNKS, 4))]
    grads = (grad_query[0], error_query[0], grad_down[0], error_down[0])
    send = call(send_kernel, [SM] + [HB] * 4, half, VM, half_bufs, 3 << 20, vmem=SEND_VMEM)(place, *grads)
    other = swap_cores(send)
    keep, qpack = call(
        keep_kernel,
        [SM] + [HB] * 6,
        (half, shape(QPAD, LANES)),
        (VM, VM),
        half_bufs + [pltpu.VMEM((2, 16, RANK), jnp.float32), dma((2,))],
        3 << 20,
        vmem=KEEP_VMEM,
    )(place, *grads, q_query.T, q_down.T)
    q_all = lax.all_gather(qpack[None], ("core", "x"), axis=0, tiled=True)
    part = exchange(keep + other, WIDE)
    part = exchange(jnp.sum(part, axis=0), NARROW)
    s_own, f = call(
        factor_kernel,
        [VM, HB],
        (shape(HALF, LANES), shape(8, PACK, LANES)),
        (VM, VM),
        [pltpu.VMEM((8, 16, LANES), jnp.float32), dma((8,))],
        1 << 18,
        vmem=FACTOR_VMEM,
    )(part, q_all)
    f = exchange(f, NARROW)
    f = jnp.broadcast_to(jnp.sum(f, axis=0)[None], (8, PACK, LANES))
    f = jnp.sum(exchange(f, WIDE), axis=0)
    both = jnp.concatenate([f, s_own], axis=0)
    both = lax.all_to_all(
        jnp.broadcast_to(both[None], (8, PACK + HALF, LANES)), ("core", "x"), 0, 0, tiled=True
    )
    basis_q, basis_d, qn_q, qn_d, approx = call(
        solve_kernel,
        [SM, VM],
        (shape(2 * QH, RANK), shape(2 * DH, RANK), shape(16, RANK), shape(16, RANK), shape(8, HALF, LANES)),
        (VM,) * 5,
        [pltpu.VMEM((2, LANES, LANES), jnp.float32)],
        1 << 20,
    )(place, both)
    approx = exchange(approx, NARROW)
    own = exchange(jnp.broadcast_to(approx[None], (8, 8, HALF, LANES)), WIDE)
    other = swap_cores(own)
    errors = (shape(2 * QH, WIDTH, dtype=bf16), shape(2 * DH, WIDTH, dtype=bf16))
    bufs = [pltpu.VMEM((n, WIDTH), bf16) for n in (QH, DH)] + [dma((CHUNKS, 2))]
    first = call(own_error_kernel, [SM] + [VM] * 5, errors, (HB, HB), bufs, 4 << 20)(place, *grads, own)
    err_q, err_d = call(
        other_error_kernel, [SM] + [VM] * 5 + [HB] * 2, errors, (HB, HB), bufs, 4 << 20, {6: 0, 7: 1}
    )(place, *grads, other, *first)
    return (err_q[None], basis_q, qn_q.T, err_d[None], basis_d, qn_d.T)


def solution(mesh):
    torus = Mesh(mesh.devices.reshape(NZ, NY, NC, NX), AXES)
    rep = ("z", "y", "core")
    big = P(rep, "x", None)
    right = P(None, AXES)
    left = P("x", None)
    return jax.shard_map(
        on_device,
        mesh=torus,
        in_specs=(big, big, right, big, big, right),
        out_specs=(big, left, right, big, left, right),
        check_vma=False,
    )
```

```python
import jax
import jax.numpy as jnp
from jax import lax
from jax.experimental import pallas as pl
from jax.experimental.pallas import tpu as pltpu
from jax.sharding import Mesh, PartitionSpec as P

NZ, NY, NC, NX = 8, 8, 2, 4
AXES = ("z", "y", "core", "x")
RANK = 64
LANES = 128
QH, DH = 16, 32
HALF = QH + DH
PACK = HALF // 2
HIGH = lax.Precision.HIGHEST
WIDTH = 8192
CHUNK = 2048
CHUNKS = WIDTH // CHUNK
MIB = 1024 * 1024


def device_of(z, y, core, x):
    return ((z * NY + y) * NC + core) * NX + x


def split_groups(core_along_y):
    groups = []
    for core in range(NC):
        for x in range(NX):
            for fixed in range(8):
                if core == core_along_y:
                    groups.append([device_of(fixed, v, core, x) for v in range(8)])
                else:
                    groups.append([device_of(v, fixed, core, x) for v in range(8)])
    return groups


WIDE = split_groups(0)
NARROW = split_groups(1)


def exchange(x, groups):
    return lax.all_to_all(x, AXES, 0, 0, axis_index_groups=groups, tiled=True)


def slot(owner, block):
    z, y = divmod(block, NY)
    return jnp.where(owner == 0, y, z), jnp.where(owner == 0, z, y)


def merge_kernel(gq, eq, gd, ed, send, keep, bq, cq, bd, cd, sems):
    f32 = jnp.float32
    copies = []
    for ch in range(CHUNKS):
        cols = pl.ds(ch * CHUNK, CHUNK)
        pairs = ((gq, bq), (eq, cq), (gd, bd), (ed, cd))
        copies.append([
            pltpu.make_async_copy(src.at[:, cols], buf.at[:, cols], sems.at[ch, a])
            for a, (src, buf) in enumerate(pairs)
        ])
        for c in copies[-1]:
            c.start()
    core = lax.axis_index("core")
    per = CHUNK // LANES
    for ch in range(CHUNKS):
        for c in copies[ch]:
            c.wait()
        for out, owner in ((send, 1 - core), (keep, core)):
            rq = pl.ds(pl.multiple_of(owner * QH, QH), QH)
            rd = pl.ds(pl.multiple_of(owner * DH, DH), DH)
            for block in range(ch * per, (ch + 1) * per):
                i, j = slot(owner, block)
                cols = pl.ds(block * LANES, LANES)
                out[i, j, 0:QH, :] = bq[rq, cols].astype(f32) + cq[rq, cols].astype(f32)
                out[i, j, QH:HALF, :] = bd[rd, cols].astype(f32) + cd[rd, cols].astype(f32)


def factor_kernel(parts, q_all, s_ref, f_ref):
    s = parts[0]
    for i in range(1, 8):
        s = s + parts[i]
    s_ref[...] = s
    q = q_all[...].reshape(LANES, LANES)
    r = jnp.dot(s, q, precision=HIGH, preferred_element_type=jnp.float32)
    low = jnp.concatenate([r[0:QH], pltpu.roll(r[40:48], RANK, 1)], axis=0)
    lane = lax.broadcasted_iota(jnp.int32, (PACK, LANES), 1)
    packed = jnp.where(lane < RANK, low, r[QH:40])
    for i in range(8):
        f_ref[i] = packed


def unpack_factor(p):
    lane_q = lax.broadcasted_iota(jnp.int32, (QH, LANES), 1)
    lane_d = lax.broadcasted_iota(jnp.int32, (DH, LANES), 1)
    fq = jnp.where(lane_q < RANK, p[0:QH], 0.0)
    fd = jnp.where(lane_d >= RANK, jnp.concatenate([p, pltpu.roll(p[QH:PACK], RANK, 1)], axis=0), 0.0)
    return fq, fd


def inverse_lower(gram):
    row = lax.broadcasted_iota(jnp.int32, (8, LANES), 0)
    lane = lax.broadcasted_iota(jnp.int32, (8, LANES), 1)
    nb = RANK // 8
    q, d = [], []
    for b in range(nb):
        eye_q = jnp.where(lane - RANK == row + 8 * b, 1.0, 0.0)
        eye_d = jnp.where(lane == row + 8 * b, 1.0, 0.0)
        q.append(jnp.where(lane < RANK, gram[8 * b:8 * b + 8], eye_q))
        d.append(jnp.where(lane >= RANK, gram[RANK + 8 * b:RANK + 8 * b + 8], eye_d))

    def spread_row(v, s):
        return jnp.broadcast_to(v[s:s + 1, :], (8, LANES))

    def spread_lane(v, at):
        return jnp.broadcast_to(v[:, at:at + 1], (8, LANES))

    for b in range(nb):
        for m, base in ((q, 0), (d, RANK)):
            at = base + 8 * b
            top = m[b]
            col = [spread_lane(top, at + t) for t in range(8)]
            below = [(i, [spread_lane(m[i], at + t) for t in range(8)]) for i in range(b + 1, nb)]
            pivots = jnp.ones((8, LANES), jnp.float32)
            for s in range(8):
                p = spread_row(col[s], s)
                pivots = jnp.where(row == s, p, pivots)
                r = 1.0 / p
                pivot_row = spread_row(top, s)
                upper = {t: spread_row(col[t], s) for t in range(s + 1, 8)}
                f = jnp.where(row > s, col[s] * r, 0.0)
                top = top - f * pivot_row
                for t in upper:
                    col[t] = col[t] - f * upper[t]
                for i, c in below:
                    g = c[s] * r
                    m[i] = m[i] - g * pivot_row
                    for t in upper:
                        c[t] = c[t] - g * upper[t]
            m[b] = top * lax.rsqrt(pivots)
    zero = jnp.zeros((8, LANES), jnp.float32)
    out = [jnp.where(lane < RANK, pltpu.roll(m, RANK, 1), zero) for m in q]
    out += [jnp.where(lane >= RANK, pltpu.roll(m, RANK, 1), zero) for m in d]
    return jnp.concatenate(out, axis=0)


def contract(a, b, dims):
    return lax.dot_general(a, b, (dims, ((), ())), precision=HIGH, preferred_element_type=jnp.float32)


def solve_kernel(all_ref, basis_q, basis_d, qn_q, qn_d, approx, qn_scratch):
    core, x = lax.axis_index("core"), lax.axis_index("x")
    f_rows, s_rows = [], []
    for g in range(8):
        fq, fd = unpack_factor(all_ref[g, 0:PACK])
        f_rows += [fq, fd]
        s_rows.append(all_ref[g, PACK:PACK + HALF])
    f = jnp.concatenate(f_rows, axis=0)
    s = jnp.concatenate(s_rows, axis=0)
    rows = ((0,), (0,))
    lanes = ((1,), (1,))
    gram = contract(f, f, rows)
    cross = contract(s, f, rows)
    inv = inverse_lower(gram)
    qn = contract(cross, inv, lanes) * (1.0 / (NZ * NY * NC))
    qn_scratch[0] = qn
    qn_scratch[1] = pltpu.roll(qn, RANK, 1)
    own = pl.ds(pl.multiple_of(core * 64 + x * 16, 16), 16)
    qn_q[...] = qn_scratch[0, own, 0:RANK]
    qn_d[...] = qn_scratch[1, own, 0:RANK]
    halves = []
    for c in range(NC):
        fq, fd = unpack_factor(all_ref[c * NX + x, 0:PACK])
        b = contract(jnp.concatenate([fq, fd], axis=0), inv, lanes)
        halves.append(b)
        basis_q[c * QH:(c + 1) * QH, :] = b[0:QH, 0:RANK]
        basis_d[c * DH:(c + 1) * DH, :] = pltpu.roll(b[QH:HALF], RANK, 1)[:, 0:RANK]
    mine = jnp.where(core == 0, halves[0], halves[1])
    a = contract(mine, qn, lanes)
    for i in range(8):
        approx[i] = a


def error_half(owner, gq, eq, gd, ed, src, out_q, out_d, buf_q, buf_d, sems):
    f32 = jnp.float32
    rq = pl.ds(pl.multiple_of(owner * QH, QH), QH)
    rd = pl.ds(pl.multiple_of(owner * DH, DH), DH)
    per = CHUNK // LANES
    copies = []
    for ch in range(CHUNKS):
        for block in range(ch * per, (ch + 1) * per):
            i, j = slot(owner, block)
            cols = pl.ds(block * LANES, LANES)
            mq = gq[rq, cols].astype(f32) + eq[rq, cols].astype(f32)
            md = gd[rd, cols].astype(f32) + ed[rd, cols].astype(f32)
            buf_q[:, cols] = (mq - src[i, j, 0:QH, :]).astype(jnp.bfloat16)
            buf_d[:, cols] = (md - src[i, j, QH:HALF, :]).astype(jnp.bfloat16)
        cols = pl.ds(ch * CHUNK, CHUNK)
        for a, (buf, out, rows) in enumerate(((buf_q, out_q, rq), (buf_d, out_d, rd))):
            c = pltpu.make_async_copy(buf.at[:, cols], out.at[rows, cols], sems.at[ch, a])
            c.start()
            copies.append(c)
    for c in copies:
        c.wait()


def own_error_kernel(gq, eq, gd, ed, src, out_q, out_d, buf_q, buf_d, sems):
    error_half(lax.axis_index("core"), gq, eq, gd, ed, src, out_q, out_d, buf_q, buf_d, sems)


def other_error_kernel(gq, eq, gd, ed, src, in_q, in_d, out_q, out_d, buf_q, buf_d, sems):
    error_half(1 - lax.axis_index("core"), gq, eq, gd, ed, src, out_q, out_d, buf_q, buf_d, sems)


def shape(*dims, dtype=jnp.float32):
    return jax.ShapeDtypeStruct(dims, dtype)


VM = pl.BlockSpec(memory_space=pltpu.VMEM)
HB = pl.BlockSpec(memory_space=pltpu.HBM)


def call(kernel, in_specs, out_shape, out_specs, scratch=(), moved=0, aliases=None):
    return pl.pallas_call(
        kernel,
        out_shape=out_shape,
        in_specs=in_specs,
        out_specs=out_specs,
        scratch_shapes=list(scratch),
        input_output_aliases=aliases or {},
        cost_estimate=pl.CostEstimate(flops=moved, bytes_accessed=moved, transcendentals=0),
        compiler_params=pltpu.CompilerParams(vmem_limit_bytes=24 * MIB),
    )


def swap_cores(x):
    return lax.ppermute(x, "core", [(0, 1), (1, 0)])


def on_device(grad_query, error_query, q_query, grad_down, error_down, q_down):
    half = shape(8, 8, HALF, LANES)
    bf16 = jnp.bfloat16
    grads = (grad_query[0], error_query[0], grad_down[0], error_down[0])
    qpack = jnp.concatenate([q_query.T, q_down.T], axis=1)
    q_all = lax.all_to_all(
        jnp.broadcast_to(qpack[None], (8, 16, LANES)), ("core", "x"), 0, 0, tiled=True
    )
    buffers = [pltpu.VMEM((n, WIDTH), bf16) for n in (2 * QH, 2 * QH, 2 * DH, 2 * DH)]
    send, keep = call(
        merge_kernel,
        [HB] * 4,
        (half, half),
        (VM, VM),
        buffers + [pltpu.SemaphoreType.DMA((CHUNKS, 4))],
        moved=6 << 20,
    )(*[pltpu.with_memory_space_constraint(g, pltpu.HBM) for g in grads])
    other = swap_cores(send)
    keep, other, q_all = lax.optimization_barrier((keep, other, q_all))
    part = exchange(keep + other, WIDE)
    part = exchange(jnp.sum(part, axis=0), NARROW)
    s_own, f = call(
        factor_kernel, [VM, VM], (shape(HALF, LANES), shape(8, PACK, LANES)), (VM, VM), moved=1 << 18
    )(part, q_all)
    f = exchange(f, NARROW)
    f = jnp.broadcast_to(jnp.sum(f, axis=0)[None], (8, PACK, LANES))
    f = jnp.sum(exchange(f, WIDE), axis=0)
    both = jnp.concatenate([f, s_own], axis=0)
    both = lax.all_to_all(
        jnp.broadcast_to(both[None], (8, PACK + HALF, LANES)), ("core", "x"), 0, 0, tiled=True
    )
    basis_q, basis_d, qn_q, qn_d, approx = call(
        solve_kernel,
        [VM],
        (shape(2 * QH, RANK), shape(2 * DH, RANK), shape(16, RANK), shape(16, RANK), shape(8, HALF, LANES)),
        (VM,) * 5,
        [pltpu.VMEM((2, LANES, LANES), jnp.float32)],
        moved=1 << 20,
    )(both)
    approx = exchange(approx, NARROW)
    own = exchange(jnp.broadcast_to(approx[None], (8, 8, HALF, LANES)), WIDE)
    other = swap_cores(own)
    errors = (shape(2 * QH, WIDTH, dtype=bf16), shape(2 * DH, WIDTH, dtype=bf16))
    bufs = [pltpu.VMEM((n, WIDTH), bf16) for n in (QH, DH)] + [pltpu.SemaphoreType.DMA((CHUNKS, 2))]
    first = call(own_error_kernel, [VM] * 5, errors, (HB, HB), bufs, 4 << 20)(*grads, own)
    err_q, err_d = call(
        other_error_kernel, [VM] * 5 + [HB] * 2, errors, (HB, HB), bufs, 4 << 20, {5: 0, 6: 1}
    )(*grads, other, *first)
    return (err_q[None], basis_q, qn_q.T, err_d[None], basis_d, qn_d.T)


def solution(mesh):
    torus = Mesh(mesh.devices.reshape(NZ, NY, NC, NX), AXES)
    rep = ("z", "y", "core")
    big = P(rep, "x", None)
    right = P(None, AXES)
    left = P("x", None)
    return jax.shard_map(
        on_device,
        mesh=torus,
        in_specs=(big, big, right, big, big, right),
        out_specs=(big, left, right, big, left, right),
        check_vma=False,
    )
```

```python
import jax
import jax.numpy as jnp
from jax import lax
from jax.experimental import pallas as pl
from jax.experimental.pallas import tpu as pltpu
from jax.sharding import Mesh, PartitionSpec as P

NZ, NY, NC, NX = 8, 8, 2, 4
AXES = ("z", "y", "core", "x")
RANK = 64
LANES = 128
QH, DH = 16, 32
HALF = QH + DH
PACK = HALF // 2
HIGH = lax.Precision.HIGHEST
WIDTH = 8192
CHUNK = 2048
CHUNKS = WIDTH // CHUNK
MIB = 1024 * 1024


def device_of(z, y, core, x):
    return ((z * NY + y) * NC + core) * NX + x


def split_groups(core_along_y):
    groups = []
    for core in range(NC):
        for x in range(NX):
            for fixed in range(8):
                if core == core_along_y:
                    groups.append([device_of(fixed, v, core, x) for v in range(8)])
                else:
                    groups.append([device_of(v, fixed, core, x) for v in range(8)])
    return groups


WIDE = split_groups(0)
NARROW = split_groups(1)


def exchange(x, groups):
    return lax.all_to_all(x, AXES, 0, 0, axis_index_groups=groups, tiled=True)


def slot(owner, block):
    z, y = divmod(block, NY)
    return jnp.where(owner == 0, y, z), jnp.where(owner == 0, z, y)


def merge_kernel(gq, eq, gd, ed, send, keep, bq, cq, bd, cd, sems):
    f32 = jnp.float32
    copies = []
    for ch in range(CHUNKS):
        cols = pl.ds(ch * CHUNK, CHUNK)
        pairs = ((gq, bq), (eq, cq), (gd, bd), (ed, cd))
        copies.append([
            pltpu.make_async_copy(src.at[:, cols], buf.at[:, cols], sems.at[ch, a])
            for a, (src, buf) in enumerate(pairs)
        ])
        for c in copies[-1]:
            c.start()
    core = lax.axis_index("core")
    per = CHUNK // LANES
    for ch in range(CHUNKS):
        for c in copies[ch]:
            c.wait()
        for out, owner in ((send, 1 - core), (keep, core)):
            rq = pl.ds(pl.multiple_of(owner * QH, QH), QH)
            rd = pl.ds(pl.multiple_of(owner * DH, DH), DH)
            for block in range(ch * per, (ch + 1) * per):
                i, j = slot(owner, block)
                cols = pl.ds(block * LANES, LANES)
                out[i, j, 0:QH, :] = bq[rq, cols].astype(f32) + cq[rq, cols].astype(f32)
                out[i, j, QH:HALF, :] = bd[rd, cols].astype(f32) + cd[rd, cols].astype(f32)


def factor_kernel(parts, q_all, s_ref, f_ref):
    s = parts[0]
    for i in range(1, 8):
        s = s + parts[i]
    s_ref[...] = s
    core, x = lax.axis_index("core"), lax.axis_index("x")
    q = [q_all[(a - x + NX) % NX, (c + core) % NC] for c in range(NC) for a in range(NX)]
    r = jnp.dot(s, jnp.concatenate(q, axis=0), precision=HIGH, preferred_element_type=jnp.float32)
    low = jnp.concatenate([r[0:QH], pltpu.roll(r[40:48], RANK, 1)], axis=0)
    lane = lax.broadcasted_iota(jnp.int32, (PACK, LANES), 1)
    packed = jnp.where(lane < RANK, low, r[QH:40])
    for i in range(8):
        f_ref[i] = packed


def unpack_factor(p):
    lane_q = lax.broadcasted_iota(jnp.int32, (QH, LANES), 1)
    lane_d = lax.broadcasted_iota(jnp.int32, (DH, LANES), 1)
    fq = jnp.where(lane_q < RANK, p[0:QH], 0.0)
    fd = jnp.where(lane_d >= RANK, jnp.concatenate([p, pltpu.roll(p[QH:PACK], RANK, 1)], axis=0), 0.0)
    return fq, fd


def inverse_lower(gram):
    row = lax.broadcasted_iota(jnp.int32, (8, LANES), 0)
    lane = lax.broadcasted_iota(jnp.int32, (8, LANES), 1)
    nb = RANK // 8
    q, d = [], []
    for b in range(nb):
        eye_q = jnp.where(lane - RANK == row + 8 * b, 1.0, 0.0)
        eye_d = jnp.where(lane == row + 8 * b, 1.0, 0.0)
        q.append(jnp.where(lane < RANK, gram[8 * b:8 * b + 8], eye_q))
        d.append(jnp.where(lane >= RANK, gram[RANK + 8 * b:RANK + 8 * b + 8], eye_d))

    def spread_row(v, s):
        return jnp.broadcast_to(v[s:s + 1, :], (8, LANES))

    def spread_lane(v, at):
        return jnp.broadcast_to(v[:, at:at + 1], (8, LANES))

    for b in range(nb):
        for m, base in ((q, 0), (d, RANK)):
            at = base + 8 * b
            top = m[b]
            col = [spread_lane(top, at + t) for t in range(8)]
            below = [(i, [spread_lane(m[i], at + t) for t in range(8)]) for i in range(b + 1, nb)]
            pivots = jnp.ones((8, LANES), jnp.float32)
            for s in range(8):
                p = spread_row(col[s], s)
                pivots = jnp.where(row == s, p, pivots)
                r = 1.0 / p
                pivot_row = spread_row(top, s)
                upper = {t: spread_row(col[t], s) for t in range(s + 1, 8)}
                f = jnp.where(row > s, col[s] * r, 0.0)
                top = top - f * pivot_row
                for t in upper:
                    col[t] = col[t] - f * upper[t]
                for i, c in below:
                    g = c[s] * r
                    m[i] = m[i] - g * pivot_row
                    for t in upper:
                        c[t] = c[t] - g * upper[t]
            m[b] = top * lax.rsqrt(pivots)
    zero = jnp.zeros((8, LANES), jnp.float32)
    out = [jnp.where(lane < RANK, pltpu.roll(m, RANK, 1), zero) for m in q]
    out += [jnp.where(lane >= RANK, pltpu.roll(m, RANK, 1), zero) for m in d]
    return jnp.concatenate(out, axis=0)


def contract(a, b, dims):
    return lax.dot_general(a, b, (dims, ((), ())), precision=HIGH, preferred_element_type=jnp.float32)


def solve_kernel(all_ref, basis_q, basis_d, qn_q, qn_d, approx, qn_scratch):
    core, x = lax.axis_index("core"), lax.axis_index("x")
    f_rows, s_rows = [], []
    for g in range(8):
        fq, fd = unpack_factor(all_ref[g, 0:PACK])
        f_rows += [fq, fd]
        s_rows.append(all_ref[g, PACK:PACK + HALF])
    f = jnp.concatenate(f_rows, axis=0)
    s = jnp.concatenate(s_rows, axis=0)
    rows = ((0,), (0,))
    lanes = ((1,), (1,))
    gram = contract(f, f, rows)
    cross = contract(s, f, rows)
    inv = inverse_lower(gram)
    qn = contract(cross, inv, lanes) * (1.0 / (NZ * NY * NC))
    qn_scratch[0] = qn
    qn_scratch[1] = pltpu.roll(qn, RANK, 1)
    own = pl.ds(pl.multiple_of(core * 64 + x * 16, 16), 16)
    qn_q[...] = qn_scratch[0, own, 0:RANK]
    qn_d[...] = qn_scratch[1, own, 0:RANK]
    halves = []
    for c in range(NC):
        fq, fd = unpack_factor(all_ref[c * NX + x, 0:PACK])
        b = contract(jnp.concatenate([fq, fd], axis=0), inv, lanes)
        halves.append(b)
        basis_q[c * QH:(c + 1) * QH, :] = b[0:QH, 0:RANK]
        basis_d[c * DH:(c + 1) * DH, :] = pltpu.roll(b[QH:HALF], RANK, 1)[:, 0:RANK]
    mine = jnp.where(core == 0, halves[0], halves[1])
    a = contract(mine, qn, lanes)
    for i in range(8):
        approx[i] = a


def error_half(owner, gq, eq, gd, ed, src, out_q, out_d, buf_q, buf_d, sems):
    f32 = jnp.float32
    rq = pl.ds(pl.multiple_of(owner * QH, QH), QH)
    rd = pl.ds(pl.multiple_of(owner * DH, DH), DH)
    per = CHUNK // LANES
    copies = []
    for ch in range(CHUNKS):
        for block in range(ch * per, (ch + 1) * per):
            i, j = slot(owner, block)
            cols = pl.ds(block * LANES, LANES)
            mq = gq[rq, cols].astype(f32) + eq[rq, cols].astype(f32)
            md = gd[rd, cols].astype(f32) + ed[rd, cols].astype(f32)
            buf_q[:, cols] = (mq - src[i, j, 0:QH, :]).astype(jnp.bfloat16)
            buf_d[:, cols] = (md - src[i, j, QH:HALF, :]).astype(jnp.bfloat16)
        cols = pl.ds(ch * CHUNK, CHUNK)
        for a, (buf, out, rows) in enumerate(((buf_q, out_q, rq), (buf_d, out_d, rd))):
            c = pltpu.make_async_copy(buf.at[:, cols], out.at[rows, cols], sems.at[ch, a])
            c.start()
            copies.append(c)
    for c in copies:
        c.wait()


def own_error_kernel(gq, eq, gd, ed, src, out_q, out_d, buf_q, buf_d, sems):
    error_half(lax.axis_index("core"), gq, eq, gd, ed, src, out_q, out_d, buf_q, buf_d, sems)


def other_error_kernel(gq, eq, gd, ed, src, in_q, in_d, out_q, out_d, buf_q, buf_d, sems):
    error_half(1 - lax.axis_index("core"), gq, eq, gd, ed, src, out_q, out_d, buf_q, buf_d, sems)


def shape(*dims, dtype=jnp.float32):
    return jax.ShapeDtypeStruct(dims, dtype)


VM = pl.BlockSpec(memory_space=pltpu.VMEM)
HB = pl.BlockSpec(memory_space=pltpu.HBM)


def call(kernel, in_specs, out_shape, out_specs, scratch=(), moved=0, aliases=None):
    return pl.pallas_call(
        kernel,
        out_shape=out_shape,
        in_specs=in_specs,
        out_specs=out_specs,
        scratch_shapes=list(scratch),
        input_output_aliases=aliases or {},
        cost_estimate=pl.CostEstimate(flops=moved, bytes_accessed=moved, transcendentals=0),
        compiler_params=pltpu.CompilerParams(vmem_limit_bytes=24 * MIB),
    )


def swap_cores(x):
    return lax.ppermute(x, "core", [(0, 1), (1, 0)])


def on_device(grad_query, error_query, q_query, grad_down, error_down, q_down):
    half = shape(8, 8, HALF, LANES)
    bf16 = jnp.bfloat16
    grads = (grad_query[0], error_query[0], grad_down[0], error_down[0])
    buffers = [pltpu.VMEM((n, WIDTH), bf16) for n in (2 * QH, 2 * QH, 2 * DH, 2 * DH)]
    send, keep = call(
        merge_kernel,
        [HB] * 4,
        (half, half),
        (VM, VM),
        buffers + [pltpu.SemaphoreType.DMA((CHUNKS, 4))],
        moved=6 << 20,
    )(*[pltpu.with_memory_space_constraint(g, pltpu.HBM) for g in grads])
    other = swap_cores(send)
    qpack = jnp.concatenate([q_query.T, q_down.T], axis=1)
    total, qpack = lax.optimization_barrier((keep + other, qpack))
    part = exchange(total, WIDE)
    qpack = jnp.stack([qpack, swap_cores(qpack)])
    q_all = jnp.stack([qpack] + [
        lax.ppermute(qpack, "x", [((x + k) % NX, x) for x in range(NX)]) for k in range(1, NX)
    ])
    part, q_all = lax.optimization_barrier((part, q_all))
    part = exchange(jnp.sum(part, axis=0), NARROW)
    s_own, f = call(
        factor_kernel, [VM, VM], (shape(HALF, LANES), shape(8, PACK, LANES)), (VM, VM), moved=1 << 18
    )(part, q_all)
    f = exchange(f, NARROW)
    f = jnp.broadcast_to(jnp.sum(f, axis=0)[None], (8, PACK, LANES))
    f = jnp.sum(exchange(f, WIDE), axis=0)
    both = jnp.concatenate([f, s_own], axis=0)
    both = lax.all_to_all(
        jnp.broadcast_to(both[None], (8, PACK + HALF, LANES)), ("core", "x"), 0, 0, tiled=True
    )
    basis_q, basis_d, qn_q, qn_d, approx = call(
        solve_kernel,
        [VM],
        (shape(2 * QH, RANK), shape(2 * DH, RANK), shape(16, RANK), shape(16, RANK), shape(8, HALF, LANES)),
        (VM,) * 5,
        [pltpu.VMEM((2, LANES, LANES), jnp.float32)],
        moved=1 << 20,
    )(both)
    approx = exchange(approx, NARROW)
    own = exchange(jnp.broadcast_to(approx[None], (8, 8, HALF, LANES)), WIDE)
    other = swap_cores(own)
    errors = (shape(2 * QH, WIDTH, dtype=bf16), shape(2 * DH, WIDTH, dtype=bf16))
    bufs = [pltpu.VMEM((n, WIDTH), bf16) for n in (QH, DH)] + [pltpu.SemaphoreType.DMA((CHUNKS, 2))]
    first = call(own_error_kernel, [VM] * 5, errors, (HB, HB), bufs, 4 << 20)(*grads, own)
    err_q, err_d = call(
        other_error_kernel, [VM] * 5 + [HB] * 2, errors, (HB, HB), bufs, 4 << 20, {5: 0, 6: 1}
    )(*grads, other, *first)
    return (err_q[None], basis_q, qn_q.T, err_d[None], basis_d, qn_d.T)


def solution(mesh):
    torus = Mesh(mesh.devices.reshape(NZ, NY, NC, NX), AXES)
    rep = ("z", "y", "core")
    big = P(rep, "x", None)
    right = P(None, AXES)
    left = P("x", None)
    return jax.shard_map(
        on_device,
        mesh=torus,
        in_specs=(big, big, right, big, big, right),
        out_specs=(big, left, right, big, left, right),
        check_vma=False,
    )
```

```python
import jax
import jax.numpy as jnp
from jax import lax
from jax.experimental import pallas as pl
from jax.experimental.pallas import tpu as pltpu
from jax.sharding import Mesh, PartitionSpec as P

NZ, NY, NC, NX = 8, 8, 2, 4
AXES = ("z", "y", "core", "x")
RANK = 64
LANES = 128
QH, DH = 16, 32
HALF = QH + DH
PACK = HALF // 2
HIGH = lax.Precision.HIGHEST
WIDTH = 8192
CHUNK = 2048
CHUNKS = WIDTH // CHUNK
MIB = 1024 * 1024


def device_of(z, y, core, x):
    return ((z * NY + y) * NC + core) * NX + x


def split_groups(core_along_y):
    groups = []
    for core in range(NC):
        for x in range(NX):
            for fixed in range(8):
                if core == core_along_y:
                    groups.append([device_of(fixed, v, core, x) for v in range(8)])
                else:
                    groups.append([device_of(v, fixed, core, x) for v in range(8)])
    return groups


WIDE = split_groups(0)
NARROW = split_groups(1)


def exchange(x, groups):
    return lax.all_to_all(x, AXES, 0, 0, axis_index_groups=groups, tiled=True)


def slot(owner, block):
    z, y = divmod(block, NY)
    return jnp.where(owner == 0, y, z), jnp.where(owner == 0, z, y)


def merge_half(owner, sources, out, bufs, sems):
    f32 = jnp.float32
    copies = []
    for ch in range(CHUNKS):
        cols = pl.ds(ch * CHUNK, CHUNK)
        part = []
        for a, (src, buf) in enumerate(zip(sources, bufs)):
            n = buf.shape[0]
            rows = pl.ds(pl.multiple_of(owner * n, n), n)
            part.append(pltpu.make_async_copy(src.at[rows, cols], buf.at[:, cols], sems.at[ch, a]))
            part[-1].start()
        copies.append(part)
    gq, eq, gd, ed = bufs
    per = CHUNK // LANES
    for ch in range(CHUNKS):
        for c in copies[ch]:
            c.wait()
        for block in range(ch * per, (ch + 1) * per):
            i, j = slot(owner, block)
            cols = pl.ds(block * LANES, LANES)
            out[i, j, 0:QH, :] = gq[:, cols].astype(f32) + eq[:, cols].astype(f32)
            out[i, j, QH:HALF, :] = gd[:, cols].astype(f32) + ed[:, cols].astype(f32)


def send_kernel(gq, eq, gd, ed, out, bq, cq, bd, cd, sems):
    merge_half(1 - lax.axis_index("core"), (gq, eq, gd, ed), out, (bq, cq, bd, cd), sems)


def keep_kernel(gq, eq, gd, ed, out, bq, cq, bd, cd, sems):
    merge_half(lax.axis_index("core"), (gq, eq, gd, ed), out, (bq, cq, bd, cd), sems)


def sum_kernel(a, b, out, buf, sems):
    copies = []
    for i in range(8):
        buf[i] = a[i] + b[i]
        copies.append(pltpu.make_async_copy(buf.at[i], out.at[i], sems.at[i]))
        copies[-1].start()
    for c in copies:
        c.wait()


def factor_kernel(parts, q_all, s_ref, f_ref):
    s = parts[0]
    for i in range(1, 8):
        s = s + parts[i]
    s_ref[...] = s
    core, x = lax.axis_index("core"), lax.axis_index("x")
    q = [q_all[(a - x + NX) % NX, (c + core) % NC] for c in range(NC) for a in range(NX)]
    r = jnp.dot(s, jnp.concatenate(q, axis=0), precision=HIGH, preferred_element_type=jnp.float32)
    low = jnp.concatenate([r[0:QH], pltpu.roll(r[40:48], RANK, 1)], axis=0)
    lane = lax.broadcasted_iota(jnp.int32, (PACK, LANES), 1)
    packed = jnp.where(lane < RANK, low, r[QH:40])
    for i in range(8):
        f_ref[i] = packed


def unpack_factor(p):
    lane_q = lax.broadcasted_iota(jnp.int32, (QH, LANES), 1)
    lane_d = lax.broadcasted_iota(jnp.int32, (DH, LANES), 1)
    fq = jnp.where(lane_q < RANK, p[0:QH], 0.0)
    fd = jnp.where(lane_d >= RANK, jnp.concatenate([p, pltpu.roll(p[QH:PACK], RANK, 1)], axis=0), 0.0)
    return fq, fd


def inverse_lower(gram):
    row = lax.broadcasted_iota(jnp.int32, (8, LANES), 0)
    lane = lax.broadcasted_iota(jnp.int32, (8, LANES), 1)
    nb = RANK // 8
    q, d = [], []
    for b in range(nb):
        eye_q = jnp.where(lane - RANK == row + 8 * b, 1.0, 0.0)
        eye_d = jnp.where(lane == row + 8 * b, 1.0, 0.0)
        q.append(jnp.where(lane < RANK, gram[8 * b:8 * b + 8], eye_q))
        d.append(jnp.where(lane >= RANK, gram[RANK + 8 * b:RANK + 8 * b + 8], eye_d))

    def spread_row(v, s):
        return jnp.broadcast_to(v[s:s + 1, :], (8, LANES))

    def spread_lane(v, at):
        return jnp.broadcast_to(v[:, at:at + 1], (8, LANES))

    for b in range(nb):
        for m, base in ((q, 0), (d, RANK)):
            at = base + 8 * b
            top = m[b]
            col = [spread_lane(top, at + t) for t in range(8)]
            below = [(i, [spread_lane(m[i], at + t) for t in range(8)]) for i in range(b + 1, nb)]
            pivots = jnp.ones((8, LANES), jnp.float32)
            for s in range(8):
                p = spread_row(col[s], s)
                pivots = jnp.where(row == s, p, pivots)
                r = 1.0 / p
                pivot_row = spread_row(top, s)
                upper = {t: spread_row(col[t], s) for t in range(s + 1, 8)}
                f = jnp.where(row > s, col[s] * r, 0.0)
                top = top - f * pivot_row
                for t in upper:
                    col[t] = col[t] - f * upper[t]
                for i, c in below:
                    g = c[s] * r
                    m[i] = m[i] - g * pivot_row
                    for t in upper:
                        c[t] = c[t] - g * upper[t]
            m[b] = top * lax.rsqrt(pivots)
    zero = jnp.zeros((8, LANES), jnp.float32)
    out = [jnp.where(lane < RANK, pltpu.roll(m, RANK, 1), zero) for m in q]
    out += [jnp.where(lane >= RANK, pltpu.roll(m, RANK, 1), zero) for m in d]
    return jnp.concatenate(out, axis=0)


def contract(a, b, dims):
    return lax.dot_general(a, b, (dims, ((), ())), precision=HIGH, preferred_element_type=jnp.float32)


def solve_kernel(all_ref, basis_q, basis_d, qn_q, qn_d, approx, qn_scratch):
    core, x = lax.axis_index("core"), lax.axis_index("x")
    f_rows, s_rows = [], []
    for g in range(8):
        fq, fd = unpack_factor(all_ref[g, 0:PACK])
        f_rows += [fq, fd]
        s_rows.append(all_ref[g, PACK:PACK + HALF])
    f = jnp.concatenate(f_rows, axis=0)
    s = jnp.concatenate(s_rows, axis=0)
    rows = ((0,), (0,))
    lanes = ((1,), (1,))
    gram = contract(f, f, rows)
    cross = contract(s, f, rows)
    inv = inverse_lower(gram)
    qn = contract(cross, inv, lanes) * (1.0 / (NZ * NY * NC))
    qn_scratch[0] = qn
    qn_scratch[1] = pltpu.roll(qn, RANK, 1)
    own = pl.ds(pl.multiple_of(core * 64 + x * 16, 16), 16)
    qn_q[...] = qn_scratch[0, own, 0:RANK]
    qn_d[...] = qn_scratch[1, own, 0:RANK]
    halves = []
    for c in range(NC):
        fq, fd = unpack_factor(all_ref[c * NX + x, 0:PACK])
        b = contract(jnp.concatenate([fq, fd], axis=0), inv, lanes)
        halves.append(b)
        basis_q[c * QH:(c + 1) * QH, :] = b[0:QH, 0:RANK]
        basis_d[c * DH:(c + 1) * DH, :] = pltpu.roll(b[QH:HALF], RANK, 1)[:, 0:RANK]
    mine = jnp.where(core == 0, halves[0], halves[1])
    a = contract(mine, qn, lanes)
    for i in range(8):
        approx[i] = a


def error_half(owner, gq, eq, gd, ed, src, out_q, out_d, buf_q, buf_d, sems):
    f32 = jnp.float32
    rq = pl.ds(pl.multiple_of(owner * QH, QH), QH)
    rd = pl.ds(pl.multiple_of(owner * DH, DH), DH)
    per = CHUNK // LANES
    copies = []
    for ch in range(CHUNKS):
        for block in range(ch * per, (ch + 1) * per):
            i, j = slot(owner, block)
            cols = pl.ds(block * LANES, LANES)
            mq = gq[rq, cols].astype(f32) + eq[rq, cols].astype(f32)
            md = gd[rd, cols].astype(f32) + ed[rd, cols].astype(f32)
            buf_q[:, cols] = (mq - src[i, j, 0:QH, :]).astype(jnp.bfloat16)
            buf_d[:, cols] = (md - src[i, j, QH:HALF, :]).astype(jnp.bfloat16)
        cols = pl.ds(ch * CHUNK, CHUNK)
        for a, (buf, out, rows) in enumerate(((buf_q, out_q, rq), (buf_d, out_d, rd))):
            c = pltpu.make_async_copy(buf.at[:, cols], out.at[rows, cols], sems.at[ch, a])
            c.start()
            copies.append(c)
    for c in copies:
        c.wait()


def own_error_kernel(gq, eq, gd, ed, src, out_q, out_d, buf_q, buf_d, sems):
    error_half(lax.axis_index("core"), gq, eq, gd, ed, src, out_q, out_d, buf_q, buf_d, sems)


def other_error_kernel(gq, eq, gd, ed, src, in_q, in_d, out_q, out_d, buf_q, buf_d, sems):
    error_half(1 - lax.axis_index("core"), gq, eq, gd, ed, src, out_q, out_d, buf_q, buf_d, sems)


def shape(*dims, dtype=jnp.float32):
    return jax.ShapeDtypeStruct(dims, dtype)


VM = pl.BlockSpec(memory_space=pltpu.VMEM)
HB = pl.BlockSpec(memory_space=pltpu.HBM)


def call(kernel, in_specs, out_shape, out_specs, scratch=(), moved=0, aliases=None):
    return pl.pallas_call(
        kernel,
        out_shape=out_shape,
        in_specs=in_specs,
        out_specs=out_specs,
        scratch_shapes=list(scratch),
        input_output_aliases=aliases or {},
        cost_estimate=pl.CostEstimate(flops=moved, bytes_accessed=moved, transcendentals=0),
        compiler_params=pltpu.CompilerParams(vmem_limit_bytes=24 * MIB),
    )


def swap_cores(x):
    return lax.ppermute(x, "core", [(0, 1), (1, 0)])


def on_device(grad_query, error_query, q_query, grad_down, error_down, q_down):
    half = shape(8, 8, HALF, LANES)
    bf16 = jnp.bfloat16
    grads = (grad_query[0], error_query[0], grad_down[0], error_down[0])
    buffers = [pltpu.VMEM((n, WIDTH), bf16) for n in (QH, QH, DH, DH)]
    buffers.append(pltpu.SemaphoreType.DMA((CHUNKS, 4)))
    pinned = [pltpu.with_memory_space_constraint(g, pltpu.HBM) for g in grads]
    other = swap_cores(call(send_kernel, [HB] * 4, half, VM, buffers, 3 << 20)(*pinned))
    keep = call(keep_kernel, [HB] * 4, half, VM, buffers, 3 << 20)(*pinned)
    staged = [pltpu.VMEM((8, 8, HALF, LANES), jnp.float32), pltpu.SemaphoreType.DMA((8,))]
    total = call(sum_kernel, [VM] * 2, half, HB, staged, 5 << 20)(keep, other)
    qpack = jnp.concatenate([q_query.T, q_down.T], axis=1)
    total, qpack = lax.optimization_barrier((total, qpack))
    part = exchange(total, WIDE)
    qpack = jnp.stack([qpack, swap_cores(qpack)])
    q_all = jnp.stack([qpack] + [
        lax.ppermute(qpack, "x", [((x + k) % NX, x) for x in range(NX)]) for k in range(1, NX)
    ])
    part, q_all = lax.optimization_barrier((part, q_all))
    part = exchange(jnp.sum(part, axis=0), NARROW)
    s_own, f = call(
        factor_kernel, [VM, VM], (shape(HALF, LANES), shape(8, PACK, LANES)), (VM, VM), moved=1 << 18
    )(part, q_all)
    f = exchange(f, NARROW)
    f = jnp.broadcast_to(jnp.sum(f, axis=0)[None], (8, PACK, LANES))
    f = jnp.sum(exchange(f, WIDE), axis=0)
    both = jnp.concatenate([f, s_own], axis=0)
    both = lax.all_to_all(
        jnp.broadcast_to(both[None], (8, PACK + HALF, LANES)), ("core", "x"), 0, 0, tiled=True
    )
    basis_q, basis_d, qn_q, qn_d, approx = call(
        solve_kernel,
        [VM],
        (shape(2 * QH, RANK), shape(2 * DH, RANK), shape(16, RANK), shape(16, RANK), shape(8, HALF, LANES)),
        (VM,) * 5,
        [pltpu.VMEM((2, LANES, LANES), jnp.float32)],
        moved=1 << 20,
    )(both)
    approx = exchange(approx, NARROW)
    own = exchange(jnp.broadcast_to(approx[None], (8, 8, HALF, LANES)), WIDE)
    other = swap_cores(own)
    errors = (shape(2 * QH, WIDTH, dtype=bf16), shape(2 * DH, WIDTH, dtype=bf16))
    bufs = [pltpu.VMEM((n, WIDTH), bf16) for n in (QH, DH)] + [pltpu.SemaphoreType.DMA((CHUNKS, 2))]
    first = call(own_error_kernel, [VM] * 5, errors, (HB, HB), bufs, 4 << 20)(*grads, own)
    err_q, err_d = call(
        other_error_kernel, [VM] * 5 + [HB] * 2, errors, (HB, HB), bufs, 4 << 20, {5: 0, 6: 1}
    )(*grads, other, *first)
    return (err_q[None], basis_q, qn_q.T, err_d[None], basis_d, qn_d.T)


def solution(mesh):
    torus = Mesh(mesh.devices.reshape(NZ, NY, NC, NX), AXES)
    rep = ("z", "y", "core")
    big = P(rep, "x", None)
    right = P(None, AXES)
    left = P("x", None)
    return jax.shard_map(
        on_device,
        mesh=torus,
        in_specs=(big, big, right, big, big, right),
        out_specs=(big, left, right, big, left, right),
        check_vma=False,
    )
```

```python
import jax
import jax.numpy as jnp
from jax import lax
from jax.experimental import pallas as pl
from jax.experimental.pallas import tpu as pltpu
from jax.sharding import Mesh, PartitionSpec as P

NZ, NY, NC, NX = 8, 8, 2, 4
AXES = ("z", "y", "core", "x")
RANK = 64
LANES = 128
QH, DH = 16, 32
HALF = QH + DH
PACK = HALF // 2
HIGH = lax.Precision.HIGHEST
WIDTH = 8192
CHUNK = 2048
CHUNKS = WIDTH // CHUNK
MIB = 1024 * 1024


def device_of(z, y, core, x):
    return ((z * NY + y) * NC + core) * NX + x


def ring_groups(core_along_y):
    groups = []
    for core in range(NC):
        for x in range(NX):
            for fixed in range(8):
                if core == core_along_y:
                    groups.append([device_of(fixed, v, core, x) for v in range(8)])
                else:
                    groups.append([device_of(v, fixed, core, x) for v in range(8)])
    return groups


def near_groups():
    groups = []
    for core in range(NC):
        for x in range(NX):
            for z in range(core, NZ + core, 2):
                for y in range(core, NY + core, 2):
                    block = [((z + i) % NZ, (y + j) % NY) for i in range(2) for j in range(2)]
                    block.sort(key=lambda zy: (zy[0] % 2, zy[1] % 2))
                    groups.append([device_of(z_, y_, core, x) for z_, y_ in block])
    return groups


def far_groups():
    return [
        [device_of(z, y, core, x) for z in range(a, NZ, 2) for y in range(b, NY, 2)]
        for core in range(NC)
        for x in range(NX)
        for a in range(2)
        for b in range(2)
    ]


RING_A = ring_groups(1)
RING_B = ring_groups(0)
NEAR = near_groups()
FAR = far_groups()


def exchange(x, groups):
    return lax.all_to_all(x, AXES, 0, 0, axis_index_groups=groups, tiled=True)


def slot(block):
    z, y = divmod(block, NY)
    return z % 2 * 2 + y % 2, z // 2 * 4 + y // 2


def merge_half(owner, sources, out, bufs, sems):
    f32 = jnp.float32
    copies = []
    for ch in range(CHUNKS):
        cols = pl.ds(ch * CHUNK, CHUNK)
        part = []
        for a, (src, buf) in enumerate(zip(sources, bufs)):
            n = buf.shape[0]
            rows = pl.ds(pl.multiple_of(owner * n, n), n)
            part.append(pltpu.make_async_copy(src.at[rows, cols], buf.at[:, cols], sems.at[ch, a]))
            part[-1].start()
        copies.append(part)
    gq, eq, gd, ed = bufs
    per = CHUNK // LANES
    for ch in range(CHUNKS):
        for c in copies[ch]:
            c.wait()
        for block in range(ch * per, (ch + 1) * per):
            i, j = slot(block)
            cols = pl.ds(block * LANES, LANES)
            out[i, j, 0:QH, :] = gq[:, cols].astype(f32) + eq[:, cols].astype(f32)
            out[i, j, QH:HALF, :] = gd[:, cols].astype(f32) + ed[:, cols].astype(f32)


def send_kernel(gq, eq, gd, ed, out, bq, cq, bd, cd, sems):
    merge_half(1 - lax.axis_index("core"), (gq, eq, gd, ed), out, (bq, cq, bd, cd), sems)


def keep_kernel(gq, eq, gd, ed, out, bq, cq, bd, cd, sems):
    merge_half(lax.axis_index("core"), (gq, eq, gd, ed), out, (bq, cq, bd, cd), sems)


def factor_kernel(parts, q_all, s_ref, f_ref):
    s = parts[0]
    for i in range(1, 16):
        s = s + parts[i]
    s_ref[...] = s
    core, x = lax.axis_index("core"), lax.axis_index("x")
    q = [q_all[(a - x + NX) % NX, (c + core) % NC] for c in range(NC) for a in range(NX)]
    r = jnp.dot(s, jnp.concatenate(q, axis=0), precision=HIGH, preferred_element_type=jnp.float32)
    low = jnp.concatenate([r[0:QH], pltpu.roll(r[40:48], RANK, 1)], axis=0)
    lane = lax.broadcasted_iota(jnp.int32, (PACK, LANES), 1)
    packed = jnp.where(lane < RANK, low, r[QH:40])
    for i in range(8):
        f_ref[i] = packed


def unpack_factor(p):
    lane_q = lax.broadcasted_iota(jnp.int32, (QH, LANES), 1)
    lane_d = lax.broadcasted_iota(jnp.int32, (DH, LANES), 1)
    fq = jnp.where(lane_q < RANK, p[0:QH], 0.0)
    fd = jnp.where(lane_d >= RANK, jnp.concatenate([p, pltpu.roll(p[QH:PACK], RANK, 1)], axis=0), 0.0)
    return fq, fd


def inverse_lower(gram):
    row = lax.broadcasted_iota(jnp.int32, (8, LANES), 0)
    lane = lax.broadcasted_iota(jnp.int32, (8, LANES), 1)
    nb = RANK // 8
    q, d = [], []
    for b in range(nb):
        eye_q = jnp.where(lane - RANK == row + 8 * b, 1.0, 0.0)
        eye_d = jnp.where(lane == row + 8 * b, 1.0, 0.0)
        q.append(jnp.where(lane < RANK, gram[8 * b:8 * b + 8], eye_q))
        d.append(jnp.where(lane >= RANK, gram[RANK + 8 * b:RANK + 8 * b + 8], eye_d))

    def spread_row(v, s):
        return jnp.broadcast_to(v[s:s + 1, :], (8, LANES))

    def spread_lane(v, at):
        return jnp.broadcast_to(v[:, at:at + 1], (8, LANES))

    for b in range(nb):
        for m, base in ((q, 0), (d, RANK)):
            at = base + 8 * b
            top = m[b]
            col = [spread_lane(top, at + t) for t in range(8)]
            below = [(i, [spread_lane(m[i], at + t) for t in range(8)]) for i in range(b + 1, nb)]
            pivots = jnp.ones((8, LANES), jnp.float32)
            for s in range(8):
                p = spread_row(col[s], s)
                pivots = jnp.where(row == s, p, pivots)
                r = 1.0 / p
                pivot_row = spread_row(top, s)
                upper = {t: spread_row(col[t], s) for t in range(s + 1, 8)}
                f = jnp.where(row > s, col[s] * r, 0.0)
                top = top - f * pivot_row
                for t in upper:
                    col[t] = col[t] - f * upper[t]
                for i, c in below:
                    g = c[s] * r
                    m[i] = m[i] - g * pivot_row
                    for t in upper:
                        c[t] = c[t] - g * upper[t]
            m[b] = top * lax.rsqrt(pivots)
    zero = jnp.zeros((8, LANES), jnp.float32)
    out = [jnp.where(lane < RANK, pltpu.roll(m, RANK, 1), zero) for m in q]
    out += [jnp.where(lane >= RANK, pltpu.roll(m, RANK, 1), zero) for m in d]
    return jnp.concatenate(out, axis=0)


def contract(a, b, dims):
    return lax.dot_general(a, b, (dims, ((), ())), precision=HIGH, preferred_element_type=jnp.float32)


def solve_kernel(all_ref, basis_q, basis_d, qn_q, qn_d, approx, qn_scratch):
    core, x = lax.axis_index("core"), lax.axis_index("x")
    f_rows, s_rows = [], []
    for g in range(8):
        fq, fd = unpack_factor(all_ref[g, 0:PACK])
        f_rows += [fq, fd]
        s_rows.append(all_ref[g, PACK:PACK + HALF])
    f = jnp.concatenate(f_rows, axis=0)
    s = jnp.concatenate(s_rows, axis=0)
    rows = ((0,), (0,))
    lanes = ((1,), (1,))
    gram = contract(f, f, rows)
    cross = contract(s, f, rows)
    inv = inverse_lower(gram)
    qn = contract(cross, inv, lanes) * (1.0 / (NZ * NY * NC))
    qn_scratch[0] = qn
    qn_scratch[1] = pltpu.roll(qn, RANK, 1)
    own = pl.ds(pl.multiple_of(core * 64 + x * 16, 16), 16)
    qn_q[...] = qn_scratch[0, own, 0:RANK]
    qn_d[...] = qn_scratch[1, own, 0:RANK]
    halves = []
    for c in range(NC):
        fq, fd = unpack_factor(all_ref[c * NX + x, 0:PACK])
        b = contract(jnp.concatenate([fq, fd], axis=0), inv, lanes)
        halves.append(b)
        basis_q[c * QH:(c + 1) * QH, :] = b[0:QH, 0:RANK]
        basis_d[c * DH:(c + 1) * DH, :] = pltpu.roll(b[QH:HALF], RANK, 1)[:, 0:RANK]
    mine = jnp.where(core == 0, halves[0], halves[1])
    a = contract(mine, qn, lanes)
    for i in range(16):
        approx[i] = a


def error_half(owner, gq, eq, gd, ed, src, out_q, out_d, buf_q, buf_d, sems):
    f32 = jnp.float32
    rq = pl.ds(pl.multiple_of(owner * QH, QH), QH)
    rd = pl.ds(pl.multiple_of(owner * DH, DH), DH)
    per = CHUNK // LANES
    copies = []
    for ch in range(CHUNKS):
        for block in range(ch * per, (ch + 1) * per):
            i, j = slot(block)
            cols = pl.ds(block * LANES, LANES)
            mq = gq[rq, cols].astype(f32) + eq[rq, cols].astype(f32)
            md = gd[rd, cols].astype(f32) + ed[rd, cols].astype(f32)
            buf_q[:, cols] = (mq - src[i, j, 0:QH, :]).astype(jnp.bfloat16)
            buf_d[:, cols] = (md - src[i, j, QH:HALF, :]).astype(jnp.bfloat16)
        cols = pl.ds(ch * CHUNK, CHUNK)
        for a, (buf, out, rows) in enumerate(((buf_q, out_q, rq), (buf_d, out_d, rd))):
            c = pltpu.make_async_copy(buf.at[:, cols], out.at[rows, cols], sems.at[ch, a])
            c.start()
            copies.append(c)
    for c in copies:
        c.wait()


def own_error_kernel(gq, eq, gd, ed, src, out_q, out_d, buf_q, buf_d, sems):
    error_half(lax.axis_index("core"), gq, eq, gd, ed, src, out_q, out_d, buf_q, buf_d, sems)


def other_error_kernel(gq, eq, gd, ed, src, in_q, in_d, out_q, out_d, buf_q, buf_d, sems):
    error_half(1 - lax.axis_index("core"), gq, eq, gd, ed, src, out_q, out_d, buf_q, buf_d, sems)


def shape(*dims, dtype=jnp.float32):
    return jax.ShapeDtypeStruct(dims, dtype)


VM = pl.BlockSpec(memory_space=pltpu.VMEM)
HB = pl.BlockSpec(memory_space=pltpu.HBM)


def call(kernel, in_specs, out_shape, out_specs, scratch=(), moved=0, aliases=None):
    return pl.pallas_call(
        kernel,
        out_shape=out_shape,
        in_specs=in_specs,
        out_specs=out_specs,
        scratch_shapes=list(scratch),
        input_output_aliases=aliases or {},
        cost_estimate=pl.CostEstimate(flops=moved, bytes_accessed=moved, transcendentals=0),
        compiler_params=pltpu.CompilerParams(vmem_limit_bytes=24 * MIB),
    )


def swap_cores(x):
    return lax.ppermute(x, "core", [(0, 1), (1, 0)])


def on_device(grad_query, error_query, q_query, grad_down, error_down, q_down):
    half = shape(4, 16, HALF, LANES)
    bf16 = jnp.bfloat16
    grads = (grad_query[0], error_query[0], grad_down[0], error_down[0])
    buffers = [pltpu.VMEM((n, WIDTH), bf16) for n in (QH, QH, DH, DH)]
    buffers.append(pltpu.SemaphoreType.DMA((CHUNKS, 4)))
    pinned = [pltpu.with_memory_space_constraint(g, pltpu.HBM) for g in grads]
    other = swap_cores(call(send_kernel, [HB] * 4, half, VM, buffers, 3 << 20)(*pinned))
    keep = call(keep_kernel, [HB] * 4, half, VM, buffers, 3 << 20)(*pinned)
    qpack = jnp.concatenate([q_query.T, q_down.T], axis=1)
    qpack = jnp.stack([qpack, swap_cores(qpack)])
    total, qpack = lax.optimization_barrier((keep + other, qpack))
    part = exchange(total, NEAR)
    q_all = jnp.stack([qpack] + [
        lax.ppermute(qpack, "x", [((x + k) % NX, x) for x in range(NX)]) for k in range(1, NX)
    ])
    part, q_all = lax.optimization_barrier((part, q_all))
    part = exchange(jnp.sum(part, axis=0), FAR)
    s_own, f = call(
        factor_kernel, [VM, VM], (shape(HALF, LANES), shape(8, PACK, LANES)), (VM, VM), moved=1 << 18
    )(part, q_all)
    f = exchange(f, RING_A)
    f = jnp.broadcast_to(jnp.sum(f, axis=0)[None], (8, PACK, LANES))
    f = jnp.sum(exchange(f, RING_B), axis=0)
    both = jnp.concatenate([f, s_own], axis=0)
    both = lax.all_to_all(
        jnp.broadcast_to(both[None], (8, PACK + HALF, LANES)), ("core", "x"), 0, 0, tiled=True
    )
    basis_q, basis_d, qn_q, qn_d, approx = call(
        solve_kernel,
        [VM],
        (shape(2 * QH, RANK), shape(2 * DH, RANK), shape(16, RANK), shape(16, RANK), shape(16, HALF, LANES)),
        (VM,) * 5,
        [pltpu.VMEM((2, LANES, LANES), jnp.float32)],
        moved=1 << 20,
    )(both)
    approx = exchange(approx, FAR)
    own = exchange(jnp.broadcast_to(approx[None], half.shape), NEAR)
    other = swap_cores(own)
    errors = (shape(2 * QH, WIDTH, dtype=bf16), shape(2 * DH, WIDTH, dtype=bf16))
    bufs = [pltpu.VMEM((n, WIDTH), bf16) for n in (QH, DH)] + [pltpu.SemaphoreType.DMA((CHUNKS, 2))]
    first = call(own_error_kernel, [VM] * 5, errors, (HB, HB), bufs, 4 << 20)(*grads, own)
    err_q, err_d = call(
        other_error_kernel, [VM] * 5 + [HB] * 2, errors, (HB, HB), bufs, 4 << 20, {5: 0, 6: 1}
    )(*grads, other, *first)
    return (err_q[None], basis_q, qn_q.T, err_d[None], basis_d, qn_d.T)


def solution(mesh):
    torus = Mesh(mesh.devices.reshape(NZ, NY, NC, NX), AXES)
    rep = ("z", "y", "core")
    big = P(rep, "x", None)
    right = P(None, AXES)
    left = P("x", None)
    return jax.shard_map(
        on_device,
        mesh=torus,
        in_specs=(big, big, right, big, big, right),
        out_specs=(big, left, right, big, left, right),
        check_vma=False,
    )
```

```python
import jax
import jax.numpy as jnp
from jax import lax
from jax.experimental import pallas as pl
from jax.experimental.pallas import tpu as pltpu
from jax.sharding import Mesh, PartitionSpec as P

NZ, NY, NC, NX = 8, 8, 2, 4
AXES = ("z", "y", "core", "x")
RANK = 64
LANES = 128
QH, DH = 16, 32
HALF = QH + DH
PACK = HALF // 2
HIGH = lax.Precision.HIGHEST
WIDTH = 8192
CHUNK = 4096
CHUNKS = WIDTH // CHUNK
ROWS = NZ * NY * HALF
MIB = 1024 * 1024


def device_of(z, y, core, x):
    return ((z * NY + y) * NC + core) * NX + x


def ring_groups(core_along_y):
    groups = []
    for core in range(NC):
        for x in range(NX):
            for fixed in range(8):
                if core == core_along_y:
                    groups.append([device_of(fixed, v, core, x) for v in range(8)])
                else:
                    groups.append([device_of(v, fixed, core, x) for v in range(8)])
    return groups


def near_groups():
    groups = []
    for core in range(NC):
        for x in range(NX):
            for z in range(core, NZ + core, 2):
                for y in range(core, NY + core, 2):
                    block = [((z + i) % NZ, (y + j) % NY) for i in range(2) for j in range(2)]
                    block.sort(key=lambda zy: (zy[0] % 2, zy[1] % 2))
                    groups.append([device_of(z_, y_, core, x) for z_, y_ in block])
    return groups


def far_groups():
    return [
        [device_of(z, y, core, x) for z in range(a, NZ, 2) for y in range(b, NY, 2)]
        for core in range(NC)
        for x in range(NX)
        for a in range(2)
        for b in range(2)
    ]


RING_A = ring_groups(1)
RING_B = ring_groups(0)
NEAR = near_groups()
FAR = far_groups()


def exchange(x, groups):
    return lax.all_to_all(x, AXES, 0, 0, axis_index_groups=groups, tiled=True)


def slot(block):
    z, y = divmod(block, NY)
    return z % 2 * 2 + y % 2, z // 2 * 4 + y // 2


def merge_half(owner, sources, out, bufs, sems):
    f32 = jnp.float32
    copies = []
    for ch in range(CHUNKS):
        cols = pl.ds(ch * CHUNK, CHUNK)
        part = []
        for a, (src, buf) in enumerate(zip(sources, bufs)):
            n = buf.shape[0]
            rows = pl.ds(pl.multiple_of(owner * n, n), n)
            part.append(pltpu.make_async_copy(src.at[rows, cols], buf.at[:, cols], sems.at[ch, a]))
            part[-1].start()
        copies.append(part)
    gq, eq, gd, ed = bufs
    per = CHUNK // LANES
    for ch in range(CHUNKS):
        for c in copies[ch]:
            c.wait()
        for block in range(ch * per, (ch + 1) * per):
            i, j = slot(block)
            at = (i * 16 + j) * HALF
            cols = pl.ds(block * LANES, LANES)
            out[at:at + QH, :] = gq[:, cols].astype(f32) + eq[:, cols].astype(f32)
            out[at + QH:at + HALF, :] = gd[:, cols].astype(f32) + ed[:, cols].astype(f32)


def send_kernel(gq, eq, gd, ed, qq, qd, out, bq, cq, bd, cd, sems, qbuf, qsems):
    copies = [pltpu.make_async_copy(r, qbuf.at[k], qsems.at[k]) for k, r in enumerate((qq, qd))]
    for c in copies:
        c.start()
    merge_half(1 - lax.axis_index("core"), (gq, eq, gd, ed), out, (bq, cq, bd, cd), sems)
    for c in copies:
        c.wait()
    out[ROWS:ROWS + 16, :] = jnp.concatenate([qbuf[0], qbuf[1]], axis=1)


def keep_kernel(gq, eq, gd, ed, out, bq, cq, bd, cd, sems):
    merge_half(lax.axis_index("core"), (gq, eq, gd, ed), out, (bq, cq, bd, cd), sems)


def factor_kernel(parts, q_all, s_ref, f_ref):
    s = parts[0]
    for i in range(1, 16):
        s = s + parts[i]
    s_ref[...] = s
    core, x = lax.axis_index("core"), lax.axis_index("x")
    q = [q_all[(a - x + NX) % NX, (c + core) % NC] for c in range(NC) for a in range(NX)]
    r = jnp.dot(s, jnp.concatenate(q, axis=0), precision=HIGH, preferred_element_type=jnp.float32)
    low = jnp.concatenate([r[0:QH], pltpu.roll(r[40:48], RANK, 1)], axis=0)
    lane = lax.broadcasted_iota(jnp.int32, (PACK, LANES), 1)
    packed = jnp.where(lane < RANK, low, r[QH:40])
    for i in range(8):
        f_ref[i] = packed


def unpack_factor(p):
    lane_q = lax.broadcasted_iota(jnp.int32, (QH, LANES), 1)
    lane_d = lax.broadcasted_iota(jnp.int32, (DH, LANES), 1)
    fq = jnp.where(lane_q < RANK, p[0:QH], 0.0)
    fd = jnp.where(lane_d >= RANK, jnp.concatenate([p, pltpu.roll(p[QH:PACK], RANK, 1)], axis=0), 0.0)
    return fq, fd


def inverse_lower(gram):
    row = lax.broadcasted_iota(jnp.int32, (8, LANES), 0)
    lane = lax.broadcasted_iota(jnp.int32, (8, LANES), 1)
    nb = RANK // 8
    q, d = [], []
    for b in range(nb):
        eye_q = jnp.where(lane - RANK == row + 8 * b, 1.0, 0.0)
        eye_d = jnp.where(lane == row + 8 * b, 1.0, 0.0)
        q.append(jnp.where(lane < RANK, gram[8 * b:8 * b + 8], eye_q))
        d.append(jnp.where(lane >= RANK, gram[RANK + 8 * b:RANK + 8 * b + 8], eye_d))

    def spread_row(v, s):
        return jnp.broadcast_to(v[s:s + 1, :], (8, LANES))

    def spread_lane(v, at):
        return jnp.broadcast_to(v[:, at:at + 1], (8, LANES))

    for b in range(nb):
        for m, base in ((q, 0), (d, RANK)):
            at = base + 8 * b
            top = m[b]
            col = [spread_lane(top, at + t) for t in range(8)]
            below = [(i, [spread_lane(m[i], at + t) for t in range(8)]) for i in range(b + 1, nb)]
            pivots = jnp.ones((8, LANES), jnp.float32)
            for s in range(8):
                p = spread_row(col[s], s)
                pivots = jnp.where(row == s, p, pivots)
                r = 1.0 / p
                pivot_row = spread_row(top, s)
                upper = {t: spread_row(col[t], s) for t in range(s + 1, 8)}
                f = jnp.where(row > s, col[s] * r, 0.0)
                top = top - f * pivot_row
                for t in upper:
                    col[t] = col[t] - f * upper[t]
                for i, c in below:
                    g = c[s] * r
                    m[i] = m[i] - g * pivot_row
                    for t in upper:
                        c[t] = c[t] - g * upper[t]
            m[b] = top * lax.rsqrt(pivots)
    zero = jnp.zeros((8, LANES), jnp.float32)
    out = [jnp.where(lane < RANK, pltpu.roll(m, RANK, 1), zero) for m in q]
    out += [jnp.where(lane >= RANK, pltpu.roll(m, RANK, 1), zero) for m in d]
    return jnp.concatenate(out, axis=0)


def contract(a, b, dims):
    return lax.dot_general(a, b, (dims, ((), ())), precision=HIGH, preferred_element_type=jnp.float32)


def solve_kernel(all_ref, basis_q, basis_d, qn_q, qn_d, approx, qn_scratch):
    core, x = lax.axis_index("core"), lax.axis_index("x")
    f_rows, s_rows = [], []
    for g in range(8):
        fq, fd = unpack_factor(all_ref[g, 0:PACK])
        f_rows += [fq, fd]
        s_rows.append(all_ref[g, PACK:PACK + HALF])
    f = jnp.concatenate(f_rows, axis=0)
    s = jnp.concatenate(s_rows, axis=0)
    rows = ((0,), (0,))
    lanes = ((1,), (1,))
    gram = contract(f, f, rows)
    cross = contract(s, f, rows)
    inv = inverse_lower(gram)
    qn = contract(cross, inv, lanes) * (1.0 / (NZ * NY * NC))
    qn_scratch[0] = qn
    qn_scratch[1] = pltpu.roll(qn, RANK, 1)
    own = pl.ds(pl.multiple_of(core * 64 + x * 16, 16), 16)
    qn_q[...] = qn_scratch[0, own, 0:RANK]
    qn_d[...] = qn_scratch[1, own, 0:RANK]
    halves = []
    for c in range(NC):
        fq, fd = unpack_factor(all_ref[c * NX + x, 0:PACK])
        b = contract(jnp.concatenate([fq, fd], axis=0), inv, lanes)
        halves.append(b)
        basis_q[c * QH:(c + 1) * QH, :] = b[0:QH, 0:RANK]
        basis_d[c * DH:(c + 1) * DH, :] = pltpu.roll(b[QH:HALF], RANK, 1)[:, 0:RANK]
    mine = jnp.where(core == 0, halves[0], halves[1])
    a = contract(mine, qn, lanes)
    for i in range(16):
        approx[i] = a


def error_half(owner, gq, eq, gd, ed, src, out_q, out_d, buf_q, buf_d, sems):
    f32 = jnp.float32
    rq = pl.ds(pl.multiple_of(owner * QH, QH), QH)
    rd = pl.ds(pl.multiple_of(owner * DH, DH), DH)
    per = CHUNK // LANES
    copies = []
    for ch in range(CHUNKS):
        for block in range(ch * per, (ch + 1) * per):
            i, j = slot(block)
            cols = pl.ds(block * LANES, LANES)
            mq = gq[rq, cols].astype(f32) + eq[rq, cols].astype(f32)
            md = gd[rd, cols].astype(f32) + ed[rd, cols].astype(f32)
            buf_q[:, cols] = (mq - src[i, j, 0:QH, :]).astype(jnp.bfloat16)
            buf_d[:, cols] = (md - src[i, j, QH:HALF, :]).astype(jnp.bfloat16)
        cols = pl.ds(ch * CHUNK, CHUNK)
        for a, (buf, out, rows) in enumerate(((buf_q, out_q, rq), (buf_d, out_d, rd))):
            c = pltpu.make_async_copy(buf.at[:, cols], out.at[rows, cols], sems.at[ch, a])
            c.start()
            copies.append(c)
    for c in copies:
        c.wait()


def own_error_kernel(gq, eq, gd, ed, src, out_q, out_d, buf_q, buf_d, sems):
    error_half(lax.axis_index("core"), gq, eq, gd, ed, src, out_q, out_d, buf_q, buf_d, sems)


def other_error_kernel(gq, eq, gd, ed, src, in_q, in_d, out_q, out_d, buf_q, buf_d, sems):
    error_half(1 - lax.axis_index("core"), gq, eq, gd, ed, src, out_q, out_d, buf_q, buf_d, sems)


def shape(*dims, dtype=jnp.float32):
    return jax.ShapeDtypeStruct(dims, dtype)


VM = pl.BlockSpec(memory_space=pltpu.VMEM)
HB = pl.BlockSpec(memory_space=pltpu.HBM)


def call(kernel, in_specs, out_shape, out_specs, scratch=(), moved=0, aliases=None):
    return pl.pallas_call(
        kernel,
        out_shape=out_shape,
        in_specs=in_specs,
        out_specs=out_specs,
        scratch_shapes=list(scratch),
        input_output_aliases=aliases or {},
        cost_estimate=pl.CostEstimate(flops=moved, bytes_accessed=moved, transcendentals=0),
        compiler_params=pltpu.CompilerParams(vmem_limit_bytes=24 * MIB),
    )


def swap_cores(x):
    return lax.ppermute(x, "core", [(0, 1), (1, 0)])


def on_device(grad_query, error_query, q_query, grad_down, error_down, q_down):
    half = shape(4, 16, HALF, LANES)
    bf16 = jnp.bfloat16
    grads = (grad_query[0], error_query[0], grad_down[0], error_down[0])
    buffers = [pltpu.VMEM((n, WIDTH), bf16) for n in (QH, QH, DH, DH)]
    buffers.append(pltpu.SemaphoreType.DMA((CHUNKS, 4)))
    pinned = [pltpu.with_memory_space_constraint(g, pltpu.HBM) for g in grads]
    pinned_q = [pltpu.with_memory_space_constraint(q.T, pltpu.HBM) for q in (q_query, q_down)]
    q_buffers = [pltpu.VMEM((2, 16, RANK), jnp.float32), pltpu.SemaphoreType.DMA((2,))]
    sent = call(
        send_kernel, [HB] * 6, shape(ROWS + 16, LANES), VM, buffers + q_buffers, moved=3 << 20
    )(*pinned, *pinned_q)
    other = swap_cores(sent)
    keep = call(keep_kernel, [HB] * 4, shape(ROWS, LANES), VM, buffers, moved=3 << 20)(*pinned)
    qpack = jnp.concatenate([q_query.T, q_down.T], axis=1)
    qpack = jnp.stack([qpack, other[ROWS:]])
    total, qpack = lax.optimization_barrier(((keep + other[:ROWS]).reshape(half.shape), qpack))
    part = exchange(total, NEAR)
    q_all = jnp.stack([qpack] + [
        lax.ppermute(qpack, "x", [((x + k) % NX, x) for x in range(NX)]) for k in range(1, NX)
    ])
    part, q_all = lax.optimization_barrier((part, q_all))
    part = exchange(jnp.sum(part, axis=0), FAR)
    s_own, f = call(
        factor_kernel, [VM, VM], (shape(HALF, LANES), shape(8, PACK, LANES)), (VM, VM), moved=1 << 18
    )(part, q_all)
    f = exchange(f, RING_A)
    f = jnp.broadcast_to(jnp.sum(f, axis=0)[None], (8, PACK, LANES))
    f = jnp.sum(exchange(f, RING_B), axis=0)
    both = jnp.concatenate([f, s_own], axis=0)
    both = lax.all_to_all(
        jnp.broadcast_to(both[None], (8, PACK + HALF, LANES)), ("core", "x"), 0, 0, tiled=True
    )
    basis_q, basis_d, qn_q, qn_d, approx = call(
        solve_kernel,
        [VM],
        (shape(2 * QH, RANK), shape(2 * DH, RANK), shape(16, RANK), shape(16, RANK), shape(16, HALF, LANES)),
        (VM,) * 5,
        [pltpu.VMEM((2, LANES, LANES), jnp.float32)],
        moved=1 << 20,
    )(both)
    approx = exchange(approx, FAR)
    own = exchange(jnp.broadcast_to(approx[None], half.shape), NEAR)
    other = swap_cores(own)
    errors = (shape(2 * QH, WIDTH, dtype=bf16), shape(2 * DH, WIDTH, dtype=bf16))
    bufs = [pltpu.VMEM((n, WIDTH), bf16) for n in (QH, DH)] + [pltpu.SemaphoreType.DMA((CHUNKS, 2))]
    first = call(own_error_kernel, [VM] * 5, errors, (HB, HB), bufs, 4 << 20)(*grads, own)
    err_q, err_d = call(
        other_error_kernel, [VM] * 5 + [HB] * 2, errors, (HB, HB), bufs, 4 << 20, {5: 0, 6: 1}
    )(*grads, other, *first)
    return (err_q[None], basis_q, qn_q.T, err_d[None], basis_d, qn_d.T)


def solution(mesh):
    torus = Mesh(mesh.devices.reshape(NZ, NY, NC, NX), AXES)
    rep = ("z", "y", "core")
    big = P(rep, "x", None)
    right = P(None, AXES)
    left = P("x", None)
    return jax.shard_map(
        on_device,
        mesh=torus,
        in_specs=(big, big, right, big, big, right),
        out_specs=(big, left, right, big, left, right),
        check_vma=False,
    )
```

```python
import jax
import jax.numpy as jnp
from jax import lax
from jax.experimental import pallas as pl
from jax.experimental.pallas import tpu as pltpu
from jax.sharding import Mesh, PartitionSpec as P

NZ, NY, NC, NX = 8, 8, 2, 4
AXES = ("z", "y", "core", "x")
RANK = 64
LANES = 128
QH, DH = 16, 32
HALF = QH + DH
PACK = HALF // 2
HIGH = lax.Precision.HIGHEST
WIDTH = 8192
CHUNK = 4096
CHUNKS = WIDTH // CHUNK
ROWS = NZ * NY * HALF
MIB = 1024 * 1024


def device_of(z, y, core, x):
    return ((z * NY + y) * NC + core) * NX + x


def ring_groups(core_along_y):
    groups = []
    for core in range(NC):
        for x in range(NX):
            for fixed in range(8):
                if core == core_along_y:
                    groups.append([device_of(fixed, v, core, x) for v in range(8)])
                else:
                    groups.append([device_of(v, fixed, core, x) for v in range(8)])
    return groups


def near_groups():
    groups = []
    for core in range(NC):
        for x in range(NX):
            for z in range(core, NZ + core, 2):
                for y in range(core, NY + core, 2):
                    block = [((z + i) % NZ, (y + j) % NY) for i in range(2) for j in range(2)]
                    block.sort(key=lambda zy: (zy[0] % 2, zy[1] % 2))
                    groups.append([device_of(z_, y_, core, x) for z_, y_ in block])
    return groups


def far_groups():
    return [
        [device_of(z, y, core, x) for z in range(a, NZ, 2) for y in range(b, NY, 2)]
        for core in range(NC)
        for x in range(NX)
        for a in range(2)
        for b in range(2)
    ]


RING_A = ring_groups(1)
RING_B = ring_groups(0)
NEAR = near_groups()
FAR = far_groups()


def exchange(x, groups):
    return lax.all_to_all(x, AXES, 0, 0, axis_index_groups=groups, tiled=True)


def slot(block):
    z, y = divmod(block, NY)
    return z % 2 * 2 + y % 2, z // 2 * 4 + y // 2


def merge_half(owner, sources, out, bufs, sems):
    f32 = jnp.float32
    copies = []
    for ch in range(CHUNKS):
        cols = pl.ds(ch * CHUNK, CHUNK)
        part = []
        for a, (src, buf) in enumerate(zip(sources, bufs)):
            n = buf.shape[0]
            rows = pl.ds(pl.multiple_of(owner * n, n), n)
            part.append(pltpu.make_async_copy(src.at[rows, cols], buf.at[:, cols], sems.at[ch, a]))
            part[-1].start()
        copies.append(part)
    gq, eq, gd, ed = bufs
    per = CHUNK // LANES
    for ch in range(CHUNKS):
        for c in copies[ch]:
            c.wait()
        for block in range(ch * per, (ch + 1) * per):
            i, j = slot(block)
            at = (i * 16 + j) * HALF
            cols = pl.ds(block * LANES, LANES)
            out[at:at + QH, :] = gq[:, cols].astype(f32) + eq[:, cols].astype(f32)
            out[at + QH:at + HALF, :] = gd[:, cols].astype(f32) + ed[:, cols].astype(f32)


def send_kernel(gq, eq, gd, ed, qq, qd, out, bq, cq, bd, cd, sems, qbuf, qsems):
    copies = [pltpu.make_async_copy(r, qbuf.at[k], qsems.at[k]) for k, r in enumerate((qq, qd))]
    for c in copies:
        c.start()
    merge_half(1 - lax.axis_index("core"), (gq, eq, gd, ed), out, (bq, cq, bd, cd), sems)
    for c in copies:
        c.wait()
    out[ROWS:ROWS + 16, :] = jnp.concatenate([qbuf[0], qbuf[1]], axis=1)


def keep_kernel(gq, eq, gd, ed, out, bq, cq, bd, cd, sems):
    merge_half(lax.axis_index("core"), (gq, eq, gd, ed), out, (bq, cq, bd, cd), sems)


def factor_kernel(parts, q_all, s_ref, f_ref):
    s = parts[0]
    for i in range(1, 16):
        s = s + parts[i]
    s_ref[...] = s
    core, x = lax.axis_index("core"), lax.axis_index("x")
    high, low = x // 2, x % 2
    q = [q_all[(a // 2 + high) % 2, (a + low) % 2, (c + core) % NC] for c in range(NC) for a in range(NX)]
    r = jnp.dot(s, jnp.concatenate(q, axis=0), precision=HIGH, preferred_element_type=jnp.float32)
    low = jnp.concatenate([r[0:QH], pltpu.roll(r[40:48], RANK, 1)], axis=0)
    lane = lax.broadcasted_iota(jnp.int32, (PACK, LANES), 1)
    packed = jnp.where(lane < RANK, low, r[QH:40])
    for i in range(8):
        f_ref[i] = packed


def unpack_factor(p):
    lane_q = lax.broadcasted_iota(jnp.int32, (QH, LANES), 1)
    lane_d = lax.broadcasted_iota(jnp.int32, (DH, LANES), 1)
    fq = jnp.where(lane_q < RANK, p[0:QH], 0.0)
    fd = jnp.where(lane_d >= RANK, jnp.concatenate([p, pltpu.roll(p[QH:PACK], RANK, 1)], axis=0), 0.0)
    return fq, fd


def inverse_lower(gram):
    row = lax.broadcasted_iota(jnp.int32, (8, LANES), 0)
    lane = lax.broadcasted_iota(jnp.int32, (8, LANES), 1)
    nb = RANK // 8
    q, d = [], []
    for b in range(nb):
        eye_q = jnp.where(lane - RANK == row + 8 * b, 1.0, 0.0)
        eye_d = jnp.where(lane == row + 8 * b, 1.0, 0.0)
        q.append(jnp.where(lane < RANK, gram[8 * b:8 * b + 8], eye_q))
        d.append(jnp.where(lane >= RANK, gram[RANK + 8 * b:RANK + 8 * b + 8], eye_d))

    def spread_row(v, s):
        return jnp.broadcast_to(v[s:s + 1, :], (8, LANES))

    def spread_lane(v, at):
        return jnp.broadcast_to(v[:, at:at + 1], (8, LANES))

    for b in range(nb):
        for m, base in ((q, 0), (d, RANK)):
            at = base + 8 * b
            top = m[b]
            col = [spread_lane(top, at + t) for t in range(8)]
            below = [(i, [spread_lane(m[i], at + t) for t in range(8)]) for i in range(b + 1, nb)]
            pivots = jnp.ones((8, LANES), jnp.float32)
            for s in range(8):
                p = spread_row(col[s], s)
                pivots = jnp.where(row == s, p, pivots)
                r = 1.0 / p
                pivot_row = spread_row(top, s)
                upper = {t: spread_row(col[t], s) for t in range(s + 1, 8)}
                f = jnp.where(row > s, col[s] * r, 0.0)
                top = top - f * pivot_row
                for t in upper:
                    col[t] = col[t] - f * upper[t]
                for i, c in below:
                    g = c[s] * r
                    m[i] = m[i] - g * pivot_row
                    for t in upper:
                        c[t] = c[t] - g * upper[t]
            m[b] = top * lax.rsqrt(pivots)
    zero = jnp.zeros((8, LANES), jnp.float32)
    out = [jnp.where(lane < RANK, pltpu.roll(m, RANK, 1), zero) for m in q]
    out += [jnp.where(lane >= RANK, pltpu.roll(m, RANK, 1), zero) for m in d]
    return jnp.concatenate(out, axis=0)


def contract(a, b, dims):
    return lax.dot_general(a, b, (dims, ((), ())), precision=HIGH, preferred_element_type=jnp.float32)


def solve_kernel(all_ref, basis_q, basis_d, qn_q, qn_d, approx, qn_scratch):
    core, x = lax.axis_index("core"), lax.axis_index("x")
    f_rows, s_rows = [], []
    for g in range(8):
        fq, fd = unpack_factor(all_ref[g, 0:PACK])
        f_rows += [fq, fd]
        s_rows.append(all_ref[g, PACK:PACK + HALF])
    f = jnp.concatenate(f_rows, axis=0)
    s = jnp.concatenate(s_rows, axis=0)
    rows = ((0,), (0,))
    lanes = ((1,), (1,))
    gram = contract(f, f, rows)
    cross = contract(s, f, rows)
    inv = inverse_lower(gram)
    qn = contract(cross, inv, lanes) * (1.0 / (NZ * NY * NC))
    qn_scratch[0] = qn
    qn_scratch[1] = pltpu.roll(qn, RANK, 1)
    own = pl.ds(pl.multiple_of(core * 64 + x * 16, 16), 16)
    qn_q[...] = qn_scratch[0, own, 0:RANK]
    qn_d[...] = qn_scratch[1, own, 0:RANK]
    halves = []
    for c in range(NC):
        fq, fd = unpack_factor(all_ref[c * NX + x, 0:PACK])
        b = contract(jnp.concatenate([fq, fd], axis=0), inv, lanes)
        halves.append(b)
        basis_q[c * QH:(c + 1) * QH, :] = b[0:QH, 0:RANK]
        basis_d[c * DH:(c + 1) * DH, :] = pltpu.roll(b[QH:HALF], RANK, 1)[:, 0:RANK]
    mine = jnp.where(core == 0, halves[0], halves[1])
    a = contract(mine, qn, lanes)
    for i in range(16):
        approx[i] = a


def error_half(owner, gq, eq, gd, ed, src, out_q, out_d, buf_q, buf_d, sems):
    f32 = jnp.float32
    rq = pl.ds(pl.multiple_of(owner * QH, QH), QH)
    rd = pl.ds(pl.multiple_of(owner * DH, DH), DH)
    per = CHUNK // LANES
    copies = []
    for ch in range(CHUNKS):
        for block in range(ch * per, (ch + 1) * per):
            i, j = slot(block)
            cols = pl.ds(block * LANES, LANES)
            mq = gq[rq, cols].astype(f32) + eq[rq, cols].astype(f32)
            md = gd[rd, cols].astype(f32) + ed[rd, cols].astype(f32)
            buf_q[:, cols] = (mq - src[i, j, 0:QH, :]).astype(jnp.bfloat16)
            buf_d[:, cols] = (md - src[i, j, QH:HALF, :]).astype(jnp.bfloat16)
        cols = pl.ds(ch * CHUNK, CHUNK)
        for a, (buf, out, rows) in enumerate(((buf_q, out_q, rq), (buf_d, out_d, rd))):
            c = pltpu.make_async_copy(buf.at[:, cols], out.at[rows, cols], sems.at[ch, a])
            c.start()
            copies.append(c)
    for c in copies:
        c.wait()


def own_error_kernel(gq, eq, gd, ed, src, out_q, out_d, buf_q, buf_d, sems):
    error_half(lax.axis_index("core"), gq, eq, gd, ed, src, out_q, out_d, buf_q, buf_d, sems)


def other_error_kernel(gq, eq, gd, ed, src, in_q, in_d, out_q, out_d, buf_q, buf_d, sems):
    error_half(1 - lax.axis_index("core"), gq, eq, gd, ed, src, out_q, out_d, buf_q, buf_d, sems)


def shape(*dims, dtype=jnp.float32):
    return jax.ShapeDtypeStruct(dims, dtype)


VM = pl.BlockSpec(memory_space=pltpu.VMEM)
HB = pl.BlockSpec(memory_space=pltpu.HBM)


def call(kernel, in_specs, out_shape, out_specs, scratch=(), moved=0, aliases=None):
    return pl.pallas_call(
        kernel,
        out_shape=out_shape,
        in_specs=in_specs,
        out_specs=out_specs,
        scratch_shapes=list(scratch),
        input_output_aliases=aliases or {},
        cost_estimate=pl.CostEstimate(flops=moved, bytes_accessed=moved, transcendentals=0),
        compiler_params=pltpu.CompilerParams(vmem_limit_bytes=24 * MIB),
    )


def swap_cores(x):
    return lax.ppermute(x, "core", [(0, 1), (1, 0)])


def on_device(grad_query, error_query, q_query, grad_down, error_down, q_down):
    half = shape(4, 16, HALF, LANES)
    bf16 = jnp.bfloat16
    grads = (grad_query[0], error_query[0], grad_down[0], error_down[0])
    buffers = [pltpu.VMEM((n, WIDTH), bf16) for n in (QH, QH, DH, DH)]
    buffers.append(pltpu.SemaphoreType.DMA((CHUNKS, 4)))
    pinned = [pltpu.with_memory_space_constraint(g, pltpu.HBM) for g in grads]
    pinned_q = [pltpu.with_memory_space_constraint(q.T, pltpu.HBM) for q in (q_query, q_down)]
    q_buffers = [pltpu.VMEM((2, 16, RANK), jnp.float32), pltpu.SemaphoreType.DMA((2,))]
    sent = call(
        send_kernel, [HB] * 6, shape(ROWS + 16, LANES), VM, buffers + q_buffers, moved=3 << 20
    )(*pinned, *pinned_q)
    other = swap_cores(sent)
    keep = call(keep_kernel, [HB] * 4, shape(ROWS, LANES), VM, buffers, moved=3 << 20)(*pinned)
    qpack = jnp.concatenate([q_query.T, q_down.T], axis=1)
    qpack = jnp.stack([qpack, other[ROWS:]])
    total, qpack = lax.optimization_barrier(((keep + other[:ROWS]).reshape(half.shape), qpack))
    part = exchange(total, NEAR)
    q_all = jnp.stack([qpack, lax.ppermute(qpack, "x", [(x, x ^ 1) for x in range(NX)])])
    q_all = jnp.stack([q_all, lax.ppermute(q_all, "x", [(x, x ^ 2) for x in range(NX)])])
    part, q_all = lax.optimization_barrier((part, q_all))
    part = exchange(jnp.sum(part, axis=0), FAR)
    s_own, f = call(
        factor_kernel, [VM, VM], (shape(HALF, LANES), shape(8, PACK, LANES)), (VM, VM), moved=1 << 18
    )(part, q_all)
    f = exchange(f, RING_A)
    f = jnp.broadcast_to(jnp.sum(f, axis=0)[None], (8, PACK, LANES))
    f = jnp.sum(exchange(f, RING_B), axis=0)
    both = jnp.concatenate([f, s_own], axis=0)
    both = lax.all_to_all(
        jnp.broadcast_to(both[None], (8, PACK + HALF, LANES)), ("core", "x"), 0, 0, tiled=True
    )
    basis_q, basis_d, qn_q, qn_d, approx = call(
        solve_kernel,
        [VM],
        (shape(2 * QH, RANK), shape(2 * DH, RANK), shape(16, RANK), shape(16, RANK), shape(16, HALF, LANES)),
        (VM,) * 5,
        [pltpu.VMEM((2, LANES, LANES), jnp.float32)],
        moved=1 << 20,
    )(both)
    approx = exchange(approx, FAR)
    own = exchange(jnp.broadcast_to(approx[None], half.shape), NEAR)
    other = swap_cores(own)
    errors = (shape(2 * QH, WIDTH, dtype=bf16), shape(2 * DH, WIDTH, dtype=bf16))
    bufs = [pltpu.VMEM((n, WIDTH), bf16) for n in (QH, DH)] + [pltpu.SemaphoreType.DMA((CHUNKS, 2))]
    first = call(own_error_kernel, [VM] * 5, errors, (HB, HB), bufs, 4 << 20)(*grads, own)
    err_q, err_d = call(
        other_error_kernel, [VM] * 5 + [HB] * 2, errors, (HB, HB), bufs, 4 << 20, {5: 0, 6: 1}
    )(*grads, other, *first)
    return (err_q[None], basis_q, qn_q.T, err_d[None], basis_d, qn_d.T)


def solution(mesh):
    torus = Mesh(mesh.devices.reshape(NZ, NY, NC, NX), AXES)
    rep = ("z", "y", "core")
    big = P(rep, "x", None)
    right = P(None, AXES)
    left = P("x", None)
    return jax.shard_map(
        on_device,
        mesh=torus,
        in_specs=(big, big, right, big, big, right),
        out_specs=(big, left, right, big, left, right),
        check_vma=False,
    )
```

```python
import jax
import jax.numpy as jnp
from jax import lax
from jax.experimental import pallas as pl
from jax.experimental.pallas import tpu as pltpu
from jax.sharding import Mesh, PartitionSpec as P

NZ, NY, NC, NX = 8, 8, 2, 4
AXES = ("z", "y", "core", "x")
RANK = 64
LANES = 128
QH, DH = 16, 32
HALF = QH + DH
PACK = HALF // 2
HIGH = lax.Precision.HIGHEST
WIDTH = 8192
CHUNK = 4096
CHUNKS = WIDTH // CHUNK
ROWS = NZ * NY * HALF
SUM_PARTS = 3
SUM_ROWS = ROWS // SUM_PARTS
MIB = 1024 * 1024


def device_of(z, y, core, x):
    return ((z * NY + y) * NC + core) * NX + x


def ring_groups(core_along_y):
    groups = []
    for core in range(NC):
        for x in range(NX):
            for fixed in range(8):
                if core == core_along_y:
                    groups.append([device_of(fixed, v, core, x) for v in range(8)])
                else:
                    groups.append([device_of(v, fixed, core, x) for v in range(8)])
    return groups


def near_groups():
    groups = []
    for core in range(NC):
        for x in range(NX):
            for z in range(core, NZ + core, 2):
                for y in range(core, NY + core, 2):
                    block = [((z + i) % NZ, (y + j) % NY) for i in range(2) for j in range(2)]
                    block.sort(key=lambda zy: (zy[0] % 2, zy[1] % 2))
                    groups.append([device_of(z_, y_, core, x) for z_, y_ in block])
    return groups


def far_groups():
    return [
        [device_of(z, y, core, x) for z in range(a, NZ, 2) for y in range(b, NY, 2)]
        for core in range(NC)
        for x in range(NX)
        for a in range(2)
        for b in range(2)
    ]


RING_A = ring_groups(1)
RING_B = ring_groups(0)
NEAR = near_groups()
FAR = far_groups()


def exchange(x, groups):
    return lax.all_to_all(x, AXES, 0, 0, axis_index_groups=groups, tiled=True)


def slot(block):
    z, y = divmod(block, NY)
    return z % 2 * 2 + y % 2, z // 2 * 4 + y // 2


def merge_half(owner, sources, out, bufs, sems):
    f32 = jnp.float32
    copies = []
    for ch in range(CHUNKS):
        cols = pl.ds(ch * CHUNK, CHUNK)
        part = []
        for a, (src, buf) in enumerate(zip(sources, bufs)):
            n = buf.shape[0]
            rows = pl.ds(pl.multiple_of(owner * n, n), n)
            part.append(pltpu.make_async_copy(src.at[rows, cols], buf.at[:, cols], sems.at[ch, a]))
            part[-1].start()
        copies.append(part)
    gq, eq, gd, ed = bufs
    per = CHUNK // LANES
    for ch in range(CHUNKS):
        for c in copies[ch]:
            c.wait()
        for block in range(ch * per, (ch + 1) * per):
            i, j = slot(block)
            at = (i * 16 + j) * HALF
            cols = pl.ds(block * LANES, LANES)
            out[at:at + QH, :] = gq[:, cols].astype(f32) + eq[:, cols].astype(f32)
            out[at + QH:at + HALF, :] = gd[:, cols].astype(f32) + ed[:, cols].astype(f32)


def send_kernel(gq, eq, gd, ed, qq, qd, out, bq, cq, bd, cd, sems, qbuf, qsems):
    copies = [pltpu.make_async_copy(r, qbuf.at[k], qsems.at[k]) for k, r in enumerate((qq, qd))]
    for c in copies:
        c.start()
    merge_half(1 - lax.axis_index("core"), (gq, eq, gd, ed), out, (bq, cq, bd, cd), sems)
    for c in copies:
        c.wait()
    out[ROWS:ROWS + 16, :] = jnp.concatenate([qbuf[0], qbuf[1]], axis=1)


def keep_kernel(gq, eq, gd, ed, out, bq, cq, bd, cd, sems):
    merge_half(lax.axis_index("core"), (gq, eq, gd, ed), out, (bq, cq, bd, cd), sems)


def sum_kernel(a, b, out, buf, sems):
    copies = []
    for k in range(SUM_PARTS):
        for i in range(k * SUM_ROWS, (k + 1) * SUM_ROWS, 256):
            part = pl.ds(i, 256)
            buf[part, :] = a[part, :] + b[part, :]
        part = pl.ds(k * SUM_ROWS, SUM_ROWS)
        copies.append(pltpu.make_async_copy(buf.at[part], out.at[part], sems.at[k]))
        copies[-1].start()
    for c in copies:
        c.wait()


def factor_kernel(parts, q_all, s_ref, f_ref):
    s = parts[0]
    for i in range(1, 16):
        s = s + parts[i]
    s_ref[...] = s
    core, x = lax.axis_index("core"), lax.axis_index("x")
    high, low = x // 2, x % 2
    q = [q_all[(a // 2 + high) % 2, (a + low) % 2, (c + core) % NC] for c in range(NC) for a in range(NX)]
    r = jnp.dot(s, jnp.concatenate(q, axis=0), precision=HIGH, preferred_element_type=jnp.float32)
    low = jnp.concatenate([r[0:QH], pltpu.roll(r[40:48], RANK, 1)], axis=0)
    lane = lax.broadcasted_iota(jnp.int32, (PACK, LANES), 1)
    packed = jnp.where(lane < RANK, low, r[QH:40])
    for i in range(8):
        f_ref[i] = packed


def unpack_factor(p):
    lane_q = lax.broadcasted_iota(jnp.int32, (QH, LANES), 1)
    lane_d = lax.broadcasted_iota(jnp.int32, (DH, LANES), 1)
    fq = jnp.where(lane_q < RANK, p[0:QH], 0.0)
    fd = jnp.where(lane_d >= RANK, jnp.concatenate([p, pltpu.roll(p[QH:PACK], RANK, 1)], axis=0), 0.0)
    return fq, fd


def inverse_lower(gram):
    row = lax.broadcasted_iota(jnp.int32, (8, LANES), 0)
    lane = lax.broadcasted_iota(jnp.int32, (8, LANES), 1)
    nb = RANK // 8
    q, d = [], []
    for b in range(nb):
        eye_q = jnp.where(lane - RANK == row + 8 * b, 1.0, 0.0)
        eye_d = jnp.where(lane == row + 8 * b, 1.0, 0.0)
        q.append(jnp.where(lane < RANK, gram[8 * b:8 * b + 8], eye_q))
        d.append(jnp.where(lane >= RANK, gram[RANK + 8 * b:RANK + 8 * b + 8], eye_d))

    def spread_row(v, s):
        return jnp.broadcast_to(v[s:s + 1, :], (8, LANES))

    def spread_lane(v, at):
        return jnp.broadcast_to(v[:, at:at + 1], (8, LANES))

    for b in range(nb):
        for m, base in ((q, 0), (d, RANK)):
            at = base + 8 * b
            top = m[b]
            col = [spread_lane(top, at + t) for t in range(8)]
            below = [(i, [spread_lane(m[i], at + t) for t in range(8)]) for i in range(b + 1, nb)]
            pivots = jnp.ones((8, LANES), jnp.float32)
            for s in range(8):
                p = spread_row(col[s], s)
                pivots = jnp.where(row == s, p, pivots)
                r = 1.0 / p
                pivot_row = spread_row(top, s)
                upper = {t: spread_row(col[t], s) for t in range(s + 1, 8)}
                f = jnp.where(row > s, col[s] * r, 0.0)
                top = top - f * pivot_row
                for t in upper:
                    col[t] = col[t] - f * upper[t]
                for i, c in below:
                    g = c[s] * r
                    m[i] = m[i] - g * pivot_row
                    for t in upper:
                        c[t] = c[t] - g * upper[t]
            m[b] = top * lax.rsqrt(pivots)
    zero = jnp.zeros((8, LANES), jnp.float32)
    out = [jnp.where(lane < RANK, pltpu.roll(m, RANK, 1), zero) for m in q]
    out += [jnp.where(lane >= RANK, pltpu.roll(m, RANK, 1), zero) for m in d]
    return jnp.concatenate(out, axis=0)


def contract(a, b, dims):
    return lax.dot_general(a, b, (dims, ((), ())), precision=HIGH, preferred_element_type=jnp.float32)


def solve_kernel(all_ref, basis_q, basis_d, qn_q, qn_d, approx, qn_scratch):
    core, x = lax.axis_index("core"), lax.axis_index("x")
    f_rows, s_rows = [], []
    for g in range(8):
        fq, fd = unpack_factor(all_ref[g, 0:PACK])
        f_rows += [fq, fd]
        s_rows.append(all_ref[g, PACK:PACK + HALF])
    f = jnp.concatenate(f_rows, axis=0)
    s = jnp.concatenate(s_rows, axis=0)
    rows = ((0,), (0,))
    lanes = ((1,), (1,))
    gram = contract(f, f, rows)
    cross = contract(s, f, rows)
    inv = inverse_lower(gram)
    qn = contract(cross, inv, lanes) * (1.0 / (NZ * NY * NC))
    qn_scratch[0] = qn
    qn_scratch[1] = pltpu.roll(qn, RANK, 1)
    own = pl.ds(pl.multiple_of(core * 64 + x * 16, 16), 16)
    qn_q[...] = qn_scratch[0, own, 0:RANK]
    qn_d[...] = qn_scratch[1, own, 0:RANK]
    halves = []
    for c in range(NC):
        fq, fd = unpack_factor(all_ref[c * NX + x, 0:PACK])
        b = contract(jnp.concatenate([fq, fd], axis=0), inv, lanes)
        halves.append(b)
        basis_q[c * QH:(c + 1) * QH, :] = b[0:QH, 0:RANK]
        basis_d[c * DH:(c + 1) * DH, :] = pltpu.roll(b[QH:HALF], RANK, 1)[:, 0:RANK]
    mine = jnp.where(core == 0, halves[0], halves[1])
    a = contract(mine, qn, lanes)
    for i in range(16):
        approx[i] = a


def error_half(owner, gq, eq, gd, ed, src, out_q, out_d, buf_q, buf_d, sems):
    f32 = jnp.float32
    rq = pl.ds(pl.multiple_of(owner * QH, QH), QH)
    rd = pl.ds(pl.multiple_of(owner * DH, DH), DH)
    per = CHUNK // LANES
    copies = []
    for ch in range(CHUNKS):
        for block in range(ch * per, (ch + 1) * per):
            i, j = slot(block)
            cols = pl.ds(block * LANES, LANES)
            mq = gq[rq, cols].astype(f32) + eq[rq, cols].astype(f32)
            md = gd[rd, cols].astype(f32) + ed[rd, cols].astype(f32)
            buf_q[:, cols] = (mq - src[i, j, 0:QH, :]).astype(jnp.bfloat16)
            buf_d[:, cols] = (md - src[i, j, QH:HALF, :]).astype(jnp.bfloat16)
        cols = pl.ds(ch * CHUNK, CHUNK)
        for a, (buf, out, rows) in enumerate(((buf_q, out_q, rq), (buf_d, out_d, rd))):
            c = pltpu.make_async_copy(buf.at[:, cols], out.at[rows, cols], sems.at[ch, a])
            c.start()
            copies.append(c)
    for c in copies:
        c.wait()


def own_error_kernel(gq, eq, gd, ed, src, out_q, out_d, buf_q, buf_d, sems):
    error_half(lax.axis_index("core"), gq, eq, gd, ed, src, out_q, out_d, buf_q, buf_d, sems)


def other_error_kernel(gq, eq, gd, ed, src, in_q, in_d, out_q, out_d, buf_q, buf_d, sems):
    error_half(1 - lax.axis_index("core"), gq, eq, gd, ed, src, out_q, out_d, buf_q, buf_d, sems)


def shape(*dims, dtype=jnp.float32):
    return jax.ShapeDtypeStruct(dims, dtype)


VM = pl.BlockSpec(memory_space=pltpu.VMEM)
HB = pl.BlockSpec(memory_space=pltpu.HBM)


def call(kernel, in_specs, out_shape, out_specs, scratch=(), moved=0, aliases=None):
    return pl.pallas_call(
        kernel,
        out_shape=out_shape,
        in_specs=in_specs,
        out_specs=out_specs,
        scratch_shapes=list(scratch),
        input_output_aliases=aliases or {},
        cost_estimate=pl.CostEstimate(flops=moved, bytes_accessed=moved, transcendentals=0),
        compiler_params=pltpu.CompilerParams(vmem_limit_bytes=24 * MIB),
    )


def swap_cores(x):
    return lax.ppermute(x, "core", [(0, 1), (1, 0)])


def on_device(grad_query, error_query, q_query, grad_down, error_down, q_down):
    half = shape(4, 16, HALF, LANES)
    bf16 = jnp.bfloat16
    grads = (grad_query[0], error_query[0], grad_down[0], error_down[0])
    buffers = [pltpu.VMEM((n, WIDTH), bf16) for n in (QH, QH, DH, DH)]
    buffers.append(pltpu.SemaphoreType.DMA((CHUNKS, 4)))
    pinned = [pltpu.with_memory_space_constraint(g, pltpu.HBM) for g in grads]
    pinned_q = [pltpu.with_memory_space_constraint(q.T, pltpu.HBM) for q in (q_query, q_down)]
    q_buffers = [pltpu.VMEM((2, 16, RANK), jnp.float32), pltpu.SemaphoreType.DMA((2,))]
    sent = call(
        send_kernel, [HB] * 6, shape(ROWS + 16, LANES), VM, buffers + q_buffers, moved=3 << 20
    )(*pinned, *pinned_q)
    other = swap_cores(sent)
    keep = call(keep_kernel, [HB] * 4, shape(ROWS, LANES), VM, buffers, moved=3 << 20)(*pinned)
    qpack = jnp.stack([sent[ROWS:], other[ROWS:]])
    staged = [pltpu.VMEM((ROWS, LANES), jnp.float32), pltpu.SemaphoreType.DMA((SUM_PARTS,))]
    total = call(sum_kernel, [VM] * 2, shape(ROWS, LANES), HB, staged, 5 << 20)(keep, other)
    total, qpack = lax.optimization_barrier((total.reshape(half.shape), qpack))
    part = exchange(total, NEAR)
    q_all = jnp.stack([qpack, lax.ppermute(qpack, "x", [(x, x ^ 1) for x in range(NX)])])
    q_all = jnp.stack([q_all, lax.ppermute(q_all, "x", [(x, x ^ 2) for x in range(NX)])])
    part, q_all = lax.optimization_barrier((part, q_all))
    part = exchange(jnp.sum(part, axis=0), FAR)
    s_own, f = call(
        factor_kernel, [VM, VM], (shape(HALF, LANES), shape(8, PACK, LANES)), (VM, VM), moved=1 << 18
    )(part, q_all)
    f = exchange(f, RING_A)
    f = jnp.broadcast_to(jnp.sum(f, axis=0)[None], (8, PACK, LANES))
    f = jnp.sum(exchange(f, RING_B), axis=0)
    both = jnp.concatenate([f, s_own], axis=0)
    both = lax.all_to_all(
        jnp.broadcast_to(both[None], (8, PACK + HALF, LANES)), ("core", "x"), 0, 0, tiled=True
    )
    basis_q, basis_d, qn_q, qn_d, approx = call(
        solve_kernel,
        [VM],
        (shape(2 * QH, RANK), shape(2 * DH, RANK), shape(16, RANK), shape(16, RANK), shape(16, HALF, LANES)),
        (VM,) * 5,
        [pltpu.VMEM((2, LANES, LANES), jnp.float32)],
        moved=1 << 20,
    )(both)
    approx = exchange(approx, FAR)
    own = exchange(jnp.broadcast_to(approx[None], half.shape), NEAR)
    other = swap_cores(own)
    errors = (shape(2 * QH, WIDTH, dtype=bf16), shape(2 * DH, WIDTH, dtype=bf16))
    bufs = [pltpu.VMEM((n, WIDTH), bf16) for n in (QH, DH)] + [pltpu.SemaphoreType.DMA((CHUNKS, 2))]
    first = call(own_error_kernel, [VM] * 5, errors, (HB, HB), bufs, 4 << 20)(*grads, own)
    err_q, err_d = call(
        other_error_kernel, [VM] * 5 + [HB] * 2, errors, (HB, HB), bufs, 4 << 20, {5: 0, 6: 1}
    )(*grads, other, *first)
    return (err_q[None], basis_q, qn_q.T, err_d[None], basis_d, qn_d.T)


def solution(mesh):
    torus = Mesh(mesh.devices.reshape(NZ, NY, NC, NX), AXES)
    rep = ("z", "y", "core")
    big = P(rep, "x", None)
    right = P(None, AXES)
    left = P("x", None)
    return jax.shard_map(
        on_device,
        mesh=torus,
        in_specs=(big, big, right, big, big, right),
        out_specs=(big, left, right, big, left, right),
        check_vma=False,
    )
```
